256 devices in a mesh: segment: 4 (over x), expert: 16 (over z, core), mp: 4 (over y).
Axes of the slice: x: 4, y: 4, z: 8, core: 2. Of those that a mesh axis runs over, the one named last changes fastest.
Arguments:
- tokens: bfloat16 [4, 2048, 4096], P('segment', 'expert', 'mp'), may hold values from -45 to 45
- routes: int32 [4, 2048, 2], P('segment', 'expert'), may hold values from 0 to 15, all different within a row; in each aligned block of 128 rows (0 to 127, 128 to 255, ..., all dimensions but the last counted through in order) at most 20 rows name the same one
- gate_weights: float32 [4, 2048, 2], P('segment', 'expert'), may hold values from 0.1 to 1
- norm_gain: float32 [4096], replicated, may hold values from 0.25 to 1.75
- gate_proj: bfloat16 [16, 4096, 7168], P('expert', None, ('segment', 'mp')), may hold values from -0.09375 to 0.09375
- up_proj: bfloat16 [16, 4096, 7168], P('expert', None, ('segment', 'mp')), may hold values from -0.09375 to 0.09375
- down_proj: bfloat16 [16, 7168, 4096], P('expert', ('segment', 'mp')), may hold values from -0.09375 to 0.09375
Outputs:
- mixed_out: bfloat16 [4, 2048, 4096], P('segment', 'expert', 'mp')
The draws below stay inside these ranges and needn't reach their ends.
Inputs may be any that keep to these rules, and one draw needn't show every extreme that they name: `routes`: the 2 experts of a token differ. In each micro-batch, each aligned block of 128 tokens (the tokens of one index of expert) names no expert more than 20 times, and in some blocks one expert exactly 20 times.
All inputs are finite; a program needn't handle non-finite values.
Results may differ from the reference program's by a relative error of at most 0.008.
Values may be sent and summed in bfloat16 or wider, within the bound.
A program may use at most 128 MiB of HBM per device.

```python
import math
import jax
import jax.numpy as jnp
import numpy as np
from jax import lax

D = 4096
HID = 7168
TOP = 2
TOK_DEV = 128
EXPERTS = 16
MICRO = 4
SEQ = 2048
CAP = 20
SECTIONS = 16


def draw_tokens(key, part):
    key = jax.random.fold_in(key, 11)
    key_rows, key_cols, key_base = jax.random.split(key, 3)
    low = math.log(0.3)
    high = math.log(3.0)
    row_scale = jnp.exp(jax.random.uniform(key_rows, (MICRO, SEQ, 1), jnp.float32, low, high))
    col_scale = jnp.exp(jax.random.uniform(key_cols, (1, 1, D), jnp.float32, low, high))
    base = jnp.clip(jax.random.normal(key_base, (MICRO, SEQ, D), jnp.float32), -4.0, 4.0)
    return (base * row_scale * col_scale).astype(jnp.bfloat16)


def strengthened(entries, own_key, source, target, shards_of, factor):
    owner, partner = [(jnp.arange(entries.shape[dim]) // (entries.shape[dim] // shards_of)).reshape([-1 if axis == dim else 1 for axis in range(entries.ndim)]) for dim in (source, target)]
    chosen = jax.random.permutation(own_key, shards_of)[partner]
    strong = (owner == chosen) | (owner == (partner + shards_of // 2) % shards_of)
    return jnp.where(strong, factor * entries, entries)


def steps_of(key, extent, cuts, low, top_value):
    def one(dim, parts):
        steps = jax.random.uniform(jax.random.fold_in(jax.random.fold_in(key, 6), dim), (parts,), jnp.float32, low / len(cuts), top_value / len(cuts))
        return jnp.repeat(jnp.exp(steps), extent[dim] // parts).reshape((-1,) + (1,) * (len(extent) - dim - 1))

    gain = one(*cuts[0])
    for cut in cuts[1:]:
        gain = gain * one(*cut)
    return gain


def assign_block(own_key, own, number, rows, count, top, limit, skew):
    order = jax.random.permutation(own_key, count)
    crowded, usual = portions_of(count, rows * top, limit, skew, True), portions_of(count, rows * top, limit, skew, False)
    places = jnp.arange(count)

    def named(sizes, turn):
        used = int((sizes > 0).sum())
        fixed = max(1, used // 4)
        passed = fixed + (places - fixed + turn * (used - fixed)) % max(1, count - fixed)
        return jnp.zeros((count,), jnp.int32).at[order[jnp.where(places < fixed, places, passed)]].set(jnp.asarray(sizes, jnp.int32))

    sizes = jnp.where(number % 4 == 0, named(crowded, number // 4), named(usual, number - number // 4 - 1))
    mixed = jax.random.permutation(jax.random.fold_in(own, 3), count)
    source_of, taker = mixed[0:count // 2 * 2:2], mixed[1:count // 2 * 2:2]
    slack = jnp.minimum(sizes[source_of] - 1, limit - sizes[taker]) // 2
    slack = jnp.where((source_of == order[0]) | (taker == order[0]) | (sizes[taker] == 0), 0, jnp.maximum(slack, 0))
    passed = jax.random.randint(jax.random.fold_in(own, 4), (count // 2,), 0, 1 << 20) % (slack + 1)
    sizes = sizes.at[source_of].add(-passed).at[taker].add(passed)
    items = jnp.searchsorted(jnp.cumsum(sizes), jnp.arange(rows * top), side="right").astype(jnp.int32)
    grid = items.reshape(top, rows).T
    grid = grid[jax.random.permutation(jax.random.fold_in(own, 1), rows)]
    turn = jax.random.randint(jax.random.fold_in(own, 2), (rows, 1), 0, top)
    return jnp.take_along_axis(grid, (jnp.arange(top)[None, :] + turn) % top, axis=1)


def portions_of(number_of, total, bound, lean, full):
    loads = [(1 << 20) // math.isqrt(grade ** lean) + 1 for grade in range(1, number_of + 1)]
    largest = bound if full else min(bound, max(-(-total // number_of), total * loads[0] // sum(loads)))
    least = 1 if total - largest >= number_of - 1 else 0
    counts, surplus = [largest] + [least] * (number_of - 1), total - largest - least * (number_of - 1)
    while surplus > 0:
        free = [i for i in range(1, number_of) if counts[i] < largest] or [i for i in range(1, number_of) if counts[i] < bound]
        whole, budget = sum([loads[i] for i in free]), surplus
        for i in free:
            extra = min(bound - counts[i], max(1, budget * loads[i] // whole), surplus)
            counts[i] = counts[i] + extra
            surplus = surplus - extra
    return np.array(counts)


def normal_values(key, extent, deviation, reach, cuts=(), held_as=jnp.bfloat16):
    drawn = jax.random.normal(key, extent, jnp.float32) * deviation
    if len(cuts) > 0:
        drawn = steps_of(key, extent, cuts, -0.22, 0.18) * drawn
    return jnp.clip(drawn, min=-reach, max=reach).astype(held_as)


def bell_draw_with(stream_key, dims, width, bound, shards, heavy, kind=jnp.bfloat16):
    entries = width * jax.random.normal(stream_key, dims, jnp.float32)
    if shards:
        entries = entries * steps_of(stream_key, dims, shards, -0.22, 0.18)
    return jnp.clip(strengthened(entries, jax.random.fold_in(stream_key, 3), *heavy), -bound, bound).astype(kind)


def setup_inputs(seed: int = 0) -> dict:
    arg_keys = jax.random.split(jax.random.key(seed), 8)
    tokens = draw_tokens(jax.random.fold_in(arg_keys[7], 71), 0)
    routes_keys = jax.random.split(jax.random.fold_in(arg_keys[1], 1), MICRO * SEQ // TOK_DEV)
    routes_turns = jax.random.permutation(jax.random.fold_in(arg_keys[1], 3), MICRO * SEQ // TOK_DEV)
    routes = jax.vmap(lambda own, number: assign_block(jax.random.fold_in(arg_keys[1], 2), own, number, TOK_DEV, EXPERTS, TOP, CAP, 2))(routes_keys, routes_turns).reshape((MICRO, SEQ, TOP))
    gate_weights = jnp.clip(0.1 + 0.9 * jax.random.uniform(arg_keys[2], (MICRO, SEQ, TOP), jnp.float32) ** steps_of(arg_keys[2], (MICRO, SEQ, TOP), ((0, 4), (1, 16)), -0.2, 0.2), 0.1, 1.0)
    norm_gain = jnp.clip(1.0 + 0.15 * jax.random.normal(arg_keys[3], (D,), jnp.float32), 0.25, 1.75)
    gate_proj = normal_values(arg_keys[4], (EXPERTS, D, HID), D ** -0.5, 0.09375, ((0, 16), (2, 16)))
    up_proj = normal_values(arg_keys[5], (EXPERTS, D, HID), D ** -0.5, 0.09375, ((0, 16), (2, 16)))
    down_proj = bell_draw_with(arg_keys[6], (EXPERTS, HID, D), HID ** -0.5, 0.09375, ((0, 16), (1, 16)), (1, 2, 16, 2.0))
    return dict(tokens=tokens, routes=routes, gate_weights=gate_weights, norm_gain=norm_gain, gate_proj=gate_proj, up_proj=up_proj, down_proj=down_proj)


EPSILON = 1e-06

def reference(tokens, routes, gate_weights, norm_gain, gate_proj, up_proj, down_proj):
    tokens_f = tokens.astype(jnp.float32)
    row_scale = lax.rsqrt(lax.optimization_barrier(jnp.mean(tokens_f * tokens_f, axis=-1, keepdims=True)) + EPSILON)
    normed = (tokens_f * row_scale * norm_gain).astype(jnp.bfloat16)
    blocks = SEQ // TOK_DEV
    block_routes = routes.reshape(MICRO, blocks, TOK_DEV * TOP)
    member = (block_routes[..., None] == jnp.arange(EXPERTS, dtype=jnp.int32)).astype(jnp.int32)
    earlier = jnp.cumsum(member, axis=2) - member
    position = lax.optimization_barrier(jnp.sum(earlier * member, axis=-1)).reshape(MICRO, blocks, TOK_DEV, TOP)
    grouped_routes = routes.reshape(MICRO, blocks, TOK_DEV, TOP)
    grouped_gates = gate_weights.reshape(MICRO, blocks, TOK_DEV, TOP)
    normed_blocks = normed.reshape(MICRO, blocks, TOK_DEV, D).astype(jnp.float32)
    slot_ids = jnp.arange(CAP, dtype=jnp.int32)
    sect_width = HID // SECTIONS

    def one_expert(running, expert):
        selector = ((grouped_routes == expert)[..., None] & (position[..., None] == slot_ids)).astype(jnp.float32)
        token_rows = jnp.einsum('mbtjc,mbtd->mbcd', selector, normed_blocks).astype(jnp.bfloat16).reshape(-1, D)
        gate_act = jnp.dot(token_rows, gate_proj[expert], preferred_element_type=jnp.float32)
        up_act = jnp.dot(token_rows, up_proj[expert], preferred_element_type=jnp.float32)
        hidden = (jax.nn.silu(gate_act) * up_act).astype(jnp.bfloat16)
        down_rows = down_proj[expert]

        def add_section(summed, section_index):
            columns = lax.dynamic_slice_in_dim(hidden, section_index * sect_width, sect_width, 1)
            weight_part = lax.dynamic_slice_in_dim(down_rows, section_index * sect_width, sect_width, 0)
            partial_value = jnp.dot(columns, weight_part, preferred_element_type=jnp.float32)
            partial_value = lax.optimization_barrier(partial_value.astype(jnp.bfloat16)).astype(jnp.float32)
            return (summed + partial_value, None)
        summed, _ = lax.scan(add_section, jnp.zeros((token_rows.shape[0], D), jnp.float32), jnp.arange(SECTIONS, dtype=jnp.int32))
        expert_out = summed.astype(jnp.bfloat16).astype(jnp.float32).reshape(MICRO, blocks, CAP, D)
        weighted = selector * grouped_gates[..., None]
        running = running + jnp.einsum('mbtjc,mbcd->mbtd', weighted, expert_out)
        return (running, None)
    mixture, _ = lax.scan(one_expert, jnp.zeros((MICRO, blocks, TOK_DEV, D), jnp.float32), jnp.arange(EXPERTS, dtype=jnp.int32))
    return (tokens_f + mixture.reshape(MICRO, SEQ, D)).astype(jnp.bfloat16)
```

```python
import functools
import jax
import jax.numpy as jnp
from jax import lax
from jax.experimental import pallas as pl
from jax.experimental.pallas import tpu as pltpu
from jax.sharding import PartitionSpec as P

EPSILON = 1e-06
SLOTS = 4
FOLDS = 4
MESH_IDS = pl.DeviceIdType.MESH

RING = (0, 1, -1, 2)
TURN = {0: -1, 1: 1, -1: -1, 2: 1}


def parent_a(dx, dy):
    if dy in (1, -1):
        return (dx, 0)
    if dy == 2:
        return (dx, TURN[dx])
    return (0, 0) if dx in (1, -1) else (1, 0)


def parent(half, node):
    dx, dy = node
    if half == 0:
        return parent_a(dx, dy)
    py, px = parent_a(dy, dx)
    return (px, py)


def level(node):
    return abs(node[0]) + abs(node[1])


NODES = [(dx, dy) for dx in RING for dy in RING if (dx, dy) != (0, 0)]
NEAR = [n for n in NODES if level(n) == 1]
FAR = [(half, n) for n in NODES if level(n) > 1 for half in (0, 1)]
NEAR_ID = {n: i for i, n in enumerate(NEAR)}
FAR_ID = {m: i for i, m in enumerate(FAR)}
IDS = len(NEAR) + len(FAR)


def children(half, node):
    return [n for h, n in FAR if h == half and parent(half, n) == node]


def depth_below(half, node):
    below = children(half, node)
    return 0 if not below else 1 + max(depth_below(half, n) for n in below)


def step_of(node, up):
    d = (up[0] - node[0], up[1] - node[1])
    return tuple({3: -1, -3: 1}.get(v, v) for v in d)


def kernel(
    dims,
    tokens_ref, routes_ref, gates_ref, gain_ref, gate_hbm, up_hbm, down_hbm,
    out_ref,
    gate_w, up_w, down_w, hidden, rows, parts, far_in, near_in,
    z_out, z_in, b_out, b_in, member, count, chosen_w, chosen_n, total, sq_out, sq_in,
    w_sem, ag_recv, rs_recv, ag_send, rs_send, z_send, z_recv, b_send, b_recv, sq_send, sq_recv,
):
    experts, segments, mps, tok, feat, chunks = dims
    f32, bf16 = jnp.float32, jnp.bfloat16
    fold = feat // FOLDS
    half_w = feat // 2
    per = FOLDS * SLOTS
    slots = experts * per
    block = experts * SLOTS
    hid = hidden.shape[1]
    seg, exp, mp = lax.axis_index("segment"), lax.axis_index("expert"), lax.axis_index("mp")

    def iota(shape, dim):
        return lax.broadcasted_iota(jnp.int32, shape, dim)

    w_copies = [
        pltpu.make_async_copy(src, dst, w_sem.at[i])
        for i, (src, dst) in enumerate(((gate_hbm, gate_w), (up_hbm, up_w), (down_hbm, down_w)))
    ]
    for copy in w_copies:
        copy.start()

    barrier = pltpu.get_barrier_semaphore()

    @pl.loop(1, experts)
    def _(d):
        pl.semaphore_signal(
            barrier, inc=1, device_id={"expert": lax.rem(exp + d, experts)}, device_id_type=MESH_IDS
        )

    for d in range(1, mps):
        pl.semaphore_signal(
            barrier, inc=1, device_id={"mp": lax.rem(mp + d, mps)}, device_id_type=MESH_IDS
        )
    for d in (1, segments - 1):
        pl.semaphore_signal(
            barrier, inc=1, device_id={"segment": lax.rem(seg + d, segments)}, device_id_type=MESH_IDS
        )

    tf = tokens_ref[...].astype(f32)
    sq = tf * tf
    folded = sq[:, 0:128]
    for i in range(1, feat // 128):
        folded = folded + sq[:, i * 128 : (i + 1) * 128]
    mine = jnp.sum(jnp.transpose(folded), axis=0, keepdims=True)
    sq_out[...] = jnp.broadcast_to(mine, (8, tok))
    total[...] = tf

    pl.semaphore_wait(barrier, experts - 1 + mps - 1 + 2)

    sq_copies = []
    for d in range(1, mps):
        copy = pltpu.make_async_remote_copy(
            src_ref=sq_out,
            dst_ref=sq_in.at[d - 1],
            send_sem=sq_send.at[d - 1],
            recv_sem=sq_recv.at[d - 1],
            device_id={"mp": lax.rem(mp + d, mps)},
            device_id_type=MESH_IDS,
        )
        copy.start()
        sq_copies.append(copy)

    row_expert = iota((slots, tok), 0) // per
    first = routes_ref[0:1, :] == row_expert
    second = routes_ref[1:2, :] == row_expert
    named = jnp.logical_or(first, second)
    before = (iota((tok, tok), 0) < iota((tok, tok), 1)).astype(bf16)
    named_f = named.astype(f32)
    earlier = jnp.dot(named_f.astype(bf16), before, preferred_element_type=f32)
    member[...] = named_f
    count[...] = jnp.where(named, earlier, -1.0)
    weight = jnp.where(first, gates_ref[0:1, :], 0.0) + jnp.where(second, gates_ref[1:2, :], 0.0)
    chosen_w[...] = jnp.transpose(weight)
    chosen_n[...] = jnp.transpose(count[...])

    for copy in sq_copies:
        copy.wait_recv()
    squares = sq_out[0:1, :]
    for d in range(mps - 1):
        squares = squares + sq_in[d, 0:1, :]
    scale = lax.rsqrt(squares / (feat * mps) + EPSILON)

    gain_tile = jnp.concatenate(
        [jnp.broadcast_to(gain_ref[mp, g : g + 1, :], (SLOTS, fold)) for g in range(FOLDS)], axis=0
    )
    gain_rows = jnp.concatenate([gain_tile] * experts, axis=0)
    row_fold = lax.rem(iota((slots, tok), 0), per) // SLOTS
    row_slot = lax.rem(iota((slots, tok), 0), SLOTS)

    def z_go(out, got, send, recv, c):
        base = pl.multiple_of(exp * per, per)
        pltpu.make_async_copy(
            out.at[c, pl.ds(base, per), :], got.at[c, pl.ds(base, per), :], recv.at[c]
        ).start()

        @pl.loop(1, experts)
        def _(d):
            other = lax.rem(exp + d, experts)
            pltpu.make_async_remote_copy(
                src_ref=out.at[c, pl.ds(pl.multiple_of(other * per, per), per), :],
                dst_ref=got.at[c, pl.ds(base, per), :],
                send_sem=send.at[c],
                recv_sem=recv.at[c],
                device_id={"expert": other},
                device_id_type=MESH_IDS,
            ).start()

    def dispatch(c):
        fill = jnp.where(count[...] == (row_slot + SLOTS * c).astype(f32), 1.0, 0.0)
        raw = jnp.zeros((slots, fold), f32)
        for g in range(FOLDS):
            pick = jnp.where(row_fold == g, fill, 0.0).astype(bf16)
            raw = raw + jnp.dot(
                pick, tokens_ref[:, g * fold : (g + 1) * fold], preferred_element_type=f32
            )
        row_scale = jnp.sum(fill * scale, axis=1, keepdims=True)
        z_out[c] = (raw * row_scale * gain_rows).astype(bf16)
        z_go(z_out, z_in, z_send, z_recv, c)

    def sign(c):
        return 1 - 2 * lax.rem(c, 2)

    def origin(c, node):
        s = sign(c)
        ox = lax.rem(seg + 2 * segments - s * node[0], segments)
        oy = lax.rem(mp + 2 * mps - s * node[1], mps)
        return ox, oy

    def spot(c, node, half=None):
        ox, oy = origin(c, node)
        r = pl.ds(pl.multiple_of(ox * block, block), block)
        if half is None:
            return r, pl.ds(pl.multiple_of(oy * feat, feat), feat)
        return r, pl.ds(pl.multiple_of(oy * feat + half * half_w, half_w), half_w)

    def hop(c, move):
        s = sign(c)
        if move[0] != 0:
            return {"segment": lax.rem(seg + segments + s * move[0], segments)}
        return {"mp": lax.rem(mp + mps + s * move[1], mps)}

    def send_near(c):
        r, f = spot(c, (0, 0))
        for node in NEAR:
            pltpu.make_async_remote_copy(
                src_ref=rows.at[c, r, f],
                dst_ref=rows.at[c, r, f],
                send_sem=ag_send.at[c],
                recv_sem=ag_recv.at[c, NEAR_ID[node]],
                device_id=hop(c, node),
                device_id_type=MESH_IDS,
            ).start()

    def wait_rows(c, lev):
        if lev == 1:
            for node in NEAR:
                r, f = spot(c, node)
                at = rows.at[c, r, f]
                pltpu.make_async_copy(at, at, ag_recv.at[c, NEAR_ID[node]]).wait()
        else:
            for half, node in FAR:
                if level(node) == lev:
                    r, f = spot(c, node, half)
                    at = rows.at[c, r, f]
                    pltpu.make_async_copy(at, at, ag_recv.at[c, len(NEAR) + FAR_ID[half, node]]).wait()

    def send_rows(c, lev):
        for half, node in FAR:
            up = parent(half, node)
            if level(up) == lev:
                r, f = spot(c, up, half)
                pltpu.make_async_remote_copy(
                    src_ref=rows.at[c, r, f],
                    dst_ref=rows.at[c, r, f],
                    send_sem=ag_send.at[c],
                    recv_sem=ag_recv.at[c, len(NEAR) + FAR_ID[half, node]],
                    device_id=hop(c, step_of(up, node)),
                    device_id_type=MESH_IDS,
                ).start()

    def unfold(c):
        pltpu.make_async_copy(z_in.at[c], z_in.at[c], z_recv.at[c]).wait()
        got = z_in[c]
        r_, q_ = iota((block, slots), 0), iota((block, slots), 1)
        place = (r_ // SLOTS) * per + lax.rem(r_, SLOTS)
        ox = pl.multiple_of(seg * block, block)
        for g in range(FOLDS):
            pick = jnp.where(q_ == place + g * SLOTS, 1.0, 0.0).astype(bf16)
            rows[c, pl.ds(ox, block), pl.ds(pl.multiple_of(mp * feat + g * fold, fold), fold)] = (
                jnp.dot(pick, got, preferred_element_type=f32).astype(bf16)
            )
        send_near(c)

    nt = (((1,), (1,)), ((), ()))

    def compute(c):
        x = rows[c]
        gate = lax.dot_general(x, gate_w[...], nt, preferred_element_type=f32)
        up = lax.dot_general(x, up_w[...], nt, preferred_element_type=f32)
        hidden[...] = (gate / (1.0 + jnp.exp(-gate)) * up).astype(bf16)

        @pl.loop(0, mps * 2)
        def _(i):
            cols = pl.ds(pl.multiple_of(i * half_w, half_w), half_w)
            parts[c, :, cols] = jnp.dot(
                hidden[...], down_w[:, cols], preferred_element_type=f32
            ).astype(bf16)

    def add_up(c, half, node):
        r, f = spot(c, node, half)
        acc = parts[c, r, f].astype(f32)
        for n in children(half, node):
            i = FAR_ID[half, n]
            at = far_in.at[c, i]
            pltpu.make_async_copy(at, at, rs_recv.at[c, len(NEAR) + i]).wait()
            acc = acc + far_in[c, i].astype(f32)
        parts[c, r, f] = acc.astype(bf16)

    def send_far(c, half, node):
        r, f = spot(c, node, half)
        i = FAR_ID[half, node]
        pltpu.make_async_remote_copy(
            src_ref=parts.at[c, r, f],
            dst_ref=far_in.at[c, i],
            send_sem=rs_send.at[c],
            recv_sem=rs_recv.at[c, len(NEAR) + i],
            device_id=hop(c, step_of(node, parent(half, node))),
            device_id_type=MESH_IDS,
        ).start()

    def sums_at(c, below):
        for half, node in FAR:
            if depth_below(half, node) == below:
                if below:
                    add_up(c, half, node)
                send_far(c, half, node)

    def sums_near(c):
        for node in NEAR:
            for half in (0, 1):
                if children(half, node):
                    add_up(c, half, node)
            r, f = spot(c, node)
            pltpu.make_async_remote_copy(
                src_ref=parts.at[c, r, f],
                dst_ref=near_in.at[c, NEAR_ID[node]],
                send_sem=rs_send.at[c],
                recv_sem=rs_recv.at[c, NEAR_ID[node]],
                device_id=hop(c, (-node[0], -node[1])),
                device_id_type=MESH_IDS,
            ).start()

    def finish(c):
        r, _ = spot(c, (0, 0))
        for i in range(len(NEAR)):
            at = near_in.at[c, i]
            pltpu.make_async_copy(at, at, rs_recv.at[c, i]).wait()
        q_, r_ = iota((slots, block), 0), iota((slots, block), 1)
        place = (r_ // SLOTS) * per + lax.rem(r_, SLOTS)
        back = jnp.zeros((slots, fold), f32)
        for g in range(FOLDS):
            acc = parts[c, r, pl.ds(pl.multiple_of(mp * feat + g * fold, fold), fold)].astype(f32)
            for i in range(len(NEAR)):
                acc = acc + near_in[c, i, :, g * fold : (g + 1) * fold].astype(f32)
            pick = jnp.where(q_ == place + g * SLOTS, 1.0, 0.0).astype(bf16)
            back = back + jnp.dot(pick, acc.astype(bf16), preferred_element_type=f32)
        b_out[c] = back.astype(bf16)
        z_go(b_out, b_in, b_send, b_recv, c)

    lane_fold = lax.rem(iota((tok, slots), 1), per) // SLOTS
    lane_slot = lax.rem(iota((tok, slots), 1), SLOTS)

    def combine(c):
        pltpu.make_async_copy(b_in.at[c], b_in.at[c], b_recv.at[c]).wait()
        got = b_in[c]
        share = jnp.where(chosen_n[...] == (lane_slot + SLOTS * c).astype(f32), chosen_w[...], 0.0)
        for g in range(FOLDS):
            part = jnp.where(lane_fold == g, share, 0.0)
            high = part.astype(bf16)
            low = (part - high.astype(f32)).astype(bf16)
            cols = slice(g * fold, (g + 1) * fold)
            total[:, cols] += jnp.dot(high, got, preferred_element_type=f32) + jnp.dot(
                low, got, preferred_element_type=f32
            )

    dispatch(0)
    dispatch(1)
    unfold(0)

    @pl.loop(2, chunks)
    def _(c):
        dispatch(c)

    for copy in w_copies:
        copy.wait()

    @pl.loop(0, chunks + 3)
    def _(t):
        def stage(lag, act):
            c = t - lag
            pl.when(jnp.logical_and(c >= 0, c < chunks))(lambda: act(c))

        @functools.partial(stage, 0)
        def _(c):
            wait_rows(c, 1)
            send_rows(c, 1)

        stage(2, sums_near)
        stage(-1, lambda c: pl.when(c >= 1)(lambda: unfold(c)))

        @functools.partial(stage, 1)
        def _(c):
            wait_rows(c, 4)
            compute(c)
            sums_at(c, 0)

        @functools.partial(stage, 0)
        def _(c):
            wait_rows(c, 2)
            send_rows(c, 2)

        stage(2, finish)
        stage(1, lambda c: sums_at(c, 1))

        @functools.partial(stage, 0)
        def _(c):
            wait_rows(c, 3)
            send_rows(c, 3)

        stage(1, lambda c: sums_at(c, 2))
        stage(3, combine)

    out_ref[...] = total[...].astype(bf16)

    for copy in sq_copies:
        copy.wait_send()
    sent = segments * mps - 1
    tall = sent * block // mps

    @pl.loop(0, chunks)
    def _(c):
        for ref, sem in ((rows, ag_send), (parts, rs_send)):
            at = ref.at[c, 0:tall, :]
            pltpu.make_async_copy(at, at, sem.at[c]).wait()
        for ref, sem in ((z_out, z_send), (b_out, b_send)):
            at = ref.at[c, 0 : slots - per, :]
            pltpu.make_async_copy(at, at, sem.at[c]).wait()


def body(tokens, routes, gate_weights, norm_gain, gate_proj, up_proj, down_proj):
    experts, segments, mps = (lax.axis_size(a) for a in ("expert", "segment", "mp"))
    tok, feat = tokens.shape[1:]
    capacity = min(tok, 20)
    chunks = -(-capacity // SLOTS)
    fold = feat // FOLDS
    slots = experts * FOLDS * SLOTS
    block = experts * SLOTS
    hid = down_proj.shape[1]
    width = feat * mps
    dims = (experts, segments, mps, tok, feat, chunks)
    bf16, f32 = jnp.bfloat16, jnp.float32
    vmem, dma = pltpu.VMEM, pltpu.SemaphoreType.DMA
    out = pl.pallas_call(
        functools.partial(kernel, dims),
        out_shape=jax.ShapeDtypeStruct((tok, feat), bf16),
        in_specs=[pl.BlockSpec(memory_space=pltpu.VMEM)] * 4 + [pl.BlockSpec(memory_space=pl.ANY)] * 3,
        out_specs=pl.BlockSpec(memory_space=pltpu.VMEM),
        scratch_shapes=[
            vmem((hid, width), bf16),
            vmem((hid, width), bf16),
            vmem((hid, width), bf16),
            vmem((segments * block, hid), bf16),
            vmem((chunks, segments * block, width), bf16),
            vmem((chunks, segments * block, width), bf16),
            vmem((chunks, len(FAR), block, feat // 2), bf16),
            vmem((chunks, len(NEAR), block, feat), bf16),
            vmem((chunks, slots, fold), bf16),
            vmem((chunks, slots, fold), bf16),
            vmem((chunks, slots, fold), bf16),
            vmem((chunks, slots, fold), bf16),
            vmem((slots, tok), f32),
            vmem((slots, tok), f32),
            vmem((tok, slots), f32),
            vmem((tok, slots), f32),
            vmem((tok, feat), f32),
            vmem((8, tok), f32),
            vmem((mps - 1, 8, tok), f32),
            dma((3,)),
            dma((chunks, IDS)),
            dma((chunks, IDS)),
            dma((chunks,)),
            dma((chunks,)),
            dma((chunks,)),
            dma((chunks,)),
            dma((chunks,)),
            dma((chunks,)),
            dma((mps - 1,)),
            dma((mps - 1,)),
        ],
        compiler_params=pltpu.CompilerParams(
            collective_id=0, has_side_effects=True, vmem_limit_bytes=60 * 1024 * 1024
        ),
        cost_estimate=pl.CostEstimate(
            flops=6 * chunks * segments * block * width * hid,
            bytes_accessed=6 * width * hid,
            transcendentals=chunks * segments * block * hid,
        ),
        name="expert_block",
    )(
        tokens[0],
        jnp.swapaxes(routes, 1, 2)[0],
        jnp.swapaxes(gate_weights, 1, 2)[0],
        norm_gain.reshape(mps, FOLDS, fold),
        jnp.swapaxes(gate_proj, 1, 2)[0],
        jnp.swapaxes(up_proj, 1, 2)[0],
        down_proj[0],
    )
    return out[None]


def solution(mesh):
    placed = (
        P("segment", "expert", "mp"),
        P("segment", "expert", None),
        P("segment", "expert", None),
        P(),
        P("expert", None, ("segment", "mp")),
        P("expert", None, ("segment", "mp")),
        P("expert", ("segment", "mp"), None),
    )
    return jax.shard_map(
        body, mesh=mesh, in_specs=placed, out_specs=P("segment", "expert", "mp"), check_vma=False
    )
```

```python
import functools
import jax
import jax.numpy as jnp
from jax import lax
from jax.experimental import pallas as pl
from jax.experimental.pallas import tpu as pltpu
from jax.sharding import PartitionSpec as P

EPSILON = 1e-06
SLOTS = 4
FOLDS = 4
MESH_IDS = pl.DeviceIdType.MESH

RING = (0, 1, -1, 2)
TURN = {0: -1, 1: 1, -1: -1, 2: 1}


def parent_a(dx, dy):
    if dy in (1, -1):
        return (dx, 0)
    if dy == 2:
        return (dx, TURN[dx])
    return (0, 0) if dx in (1, -1) else (1, 0)


def parent(half, node):
    dx, dy = node
    if half == 0:
        return parent_a(dx, dy)
    py, px = parent_a(dy, dx)
    return (px, py)


def level(node):
    return abs(node[0]) + abs(node[1])


NODES = [(dx, dy) for dx in RING for dy in RING if (dx, dy) != (0, 0)]
NEAR = [n for n in NODES if level(n) == 1]
FAR = [(half, n) for n in NODES if level(n) > 1 for half in (0, 1)]
NEAR_ID = {n: i for i, n in enumerate(NEAR)}
FAR_ID = {m: i for i, m in enumerate(FAR)}
IDS = len(NEAR) + len(FAR)


def children(half, node):
    return [n for h, n in FAR if h == half and parent(half, n) == node]


def depth_below(half, node):
    below = children(half, node)
    return 0 if not below else 1 + max(depth_below(half, n) for n in below)


def step_of(node, up):
    d = (up[0] - node[0], up[1] - node[1])
    return tuple({3: -1, -3: 1}.get(v, v) for v in d)


ORDER = (
    ("z", 0), ("z", 1), ("fold",), ("uf", 0), ("uf", 1), ("z", 2), ("z", 3), ("fn", 0, (0, 1)),
    ("fn", 0, (0, -1)), ("fn", 0, (1, 0)), ("fn", 0, (-1, 0)), ("z", 4), ("fn", 1, (0, -1)), ("fn", 1, (0, 1)),
    ("ff", 0, 1, (0, 2)), ("ff", 0, 1, (1, 1)), ("fn", 1, (1, 0)), ("ff", 0, 0, (1, 1)), ("ff", 0, 1, (-1, -1)),
    ("fn", 1, (-1, 0)), ("ff", 0, 0, (-1, -1)), ("ff", 0, 0, (2, 0)), ("ff", 1, 1, (0, 2)),
    ("ff", 1, 1, (-1, -1)), ("ff", 1, 0, (1, 1)), ("ff", 1, 1, (1, 1)), ("uf", 2), ("ff", 0, 1, (1, 2)),
    ("ff", 1, 0, (-1, -1)), ("ff", 1, 0, (2, 0)), ("ff", 0, 0, (2, 1)), ("uf", 3), ("ff", 1, 1, (1, 2)),
    ("uf", 4), ("fn", 2, (0, 1)), ("fn", 2, (0, -1)), ("ff", 1, 0, (2, 1)), ("fn", 2, (1, 0)),
    ("fn", 2, (-1, 0)), ("gu", 0), ("dn", 0, 2), ("dn", 0, 1), ("dn", 0, -1), ("dn", 0, 0),
    ("ff", 2, 1, (0, 2)), ("ff", 2, 1, (1, 1)), ("fn", 3, (0, 1)), ("ff", 2, 0, (1, 1)), ("ff", 2, 1, (-1, -1)),
    ("fn", 3, (0, -1)), ("ff", 2, 0, (-1, -1)), ("ff", 2, 0, (2, 0)), ("fn", 3, (1, 0)), ("fn", 3, (-1, 0)),
    ("gu", 1), ("dn", 1, 2), ("dn", 1, 1), ("dn", 1, -1), ("dn", 1, 0), ("ff", 3, 1, (0, 2)),
    ("ff", 3, 1, (1, 1)), ("ff", 2, 1, (1, 2)), ("rf", 0, 1, (1, 2)), ("rf", 0, 0, (1, 1)),
    ("rf", 0, 1, (1, 1)), ("rf", 0, 0, (2, 1)), ("rf", 0, 0, (-1, -1)), ("rf", 0, 1, (-1, -1)),
    ("ff", 3, 0, (1, 1)), ("ff", 2, 0, (2, 1)), ("fn", 4, (0, 1)), ("ff", 3, 1, (-1, -1)), ("ff", 3, 0, (2, 0)),
    ("ff", 3, 0, (-1, -1)), ("fn", 4, (0, -1)), ("fn", 4, (1, 0)), ("fn", 4, (-1, 0)), ("rf", 1, 0, (1, 1)),
    ("rf", 1, 1, (1, 2)), ("rf", 1, 0, (-1, -1)), ("rf", 1, 0, (2, 1)), ("rf", 1, 1, (1, 1)),
    ("rf", 1, 1, (-1, -1)), ("ff", 3, 1, (1, 2)), ("rn", 0, (-1, 0)), ("rf", 0, 0, (2, 0)),
    ("ff", 4, 1, (0, 2)), ("rf", 0, 1, (0, 2)), ("rn", 0, (0, -1)), ("ff", 4, 1, (1, 1)), ("ff", 3, 0, (2, 1)),
    ("gu", 2), ("dn", 2, 2), ("dn", 2, 1), ("dn", 2, -1), ("dn", 2, 0), ("ff", 4, 0, (1, 1)),
    ("ff", 4, 0, (-1, -1)), ("ff", 4, 1, (-1, -1)), ("ff", 4, 0, (2, 0)), ("rf", 1, 1, (0, 2)),
    ("rf", 1, 0, (2, 0)), ("rn", 0, (0, 1)), ("rn", 0, (1, 0)), ("rn", 1, (0, -1)), ("rf", 2, 0, (1, 1)),
    ("rn", 1, (-1, 0)), ("ff", 4, 1, (1, 2)), ("rf", 2, 1, (1, 2)), ("rf", 2, 0, (2, 1)), ("gu", 3),
    ("dn", 3, 2), ("dn", 3, 1), ("dn", 3, -1), ("dn", 3, 0), ("ff", 4, 0, (2, 1)), ("rf", 2, 1, (1, 1)),
    ("rf", 2, 0, (-1, -1)), ("rf", 2, 1, (-1, -1)), ("fi", 0), ("rf", 3, 0, (1, 1)), ("rn", 1, (0, 1)),
    ("rn", 1, (1, 0)), ("rf", 2, 1, (0, 2)), ("rf", 3, 1, (1, 2)), ("rf", 3, 0, (2, 1)), ("rf", 2, 0, (2, 0)),
    ("rf", 3, 1, (1, 1)), ("gu", 4), ("dn", 4, 2), ("dn", 4, 1), ("dn", 4, -1), ("dn", 4, 0),
    ("rf", 3, 1, (0, 2)), ("rf", 3, 0, (-1, -1)), ("rf", 3, 1, (-1, -1)), ("rf", 3, 0, (2, 0)), ("fi", 1),
    ("rf", 4, 1, (1, 2)), ("rf", 4, 0, (1, 1)), ("rf", 4, 1, (1, 1)), ("rf", 4, 0, (2, 1)),
    ("rf", 4, 0, (-1, -1)), ("rn", 2, (0, 1)), ("rf", 4, 1, (-1, -1)), ("rn", 2, (0, -1)), ("rn", 2, (1, 0)),
    ("rf", 4, 1, (0, 2)), ("rn", 2, (-1, 0)), ("rf", 4, 0, (2, 0)), ("rn", 3, (0, 1)), ("rn", 3, (0, -1)),
    ("rn", 3, (1, 0)), ("rn", 3, (-1, 0)), ("rn", 4, (0, -1)), ("rn", 4, (-1, 0)), ("fi", 2), ("rn", 4, (0, 1)),
    ("rn", 4, (1, 0)), ("fi", 3), ("fi", 4), ("co", 0), ("co", 1), ("co", 2), ("co", 3), ("co", 4),
)


def kernel(
    dims,
    tokens_ref, routes_ref, gates_ref, gain_ref, gate_hbm, up_hbm, down_hbm,
    out_ref,
    gate_w, up_w, down_w, hidden, rows, parts, far_in, near_in,
    z_out, z_in, b_out, b_in, count, chosen_w, chosen_n, total,
    w_sem, ag_recv, rs_recv, ag_send, rs_send, z_send, z_recv, b_send, b_recv,
):
    experts, segments, mps, tok, feat, chunks = dims
    f32, bf16 = jnp.float32, jnp.bfloat16
    fold = feat // FOLDS
    half_w = feat // 2
    per = FOLDS * SLOTS
    slots = experts * per
    block = experts * SLOTS
    seg, exp, mp = lax.axis_index("segment"), lax.axis_index("expert"), lax.axis_index("mp")

    def iota(shape, dim):
        return lax.broadcasted_iota(jnp.int32, shape, dim)

    barrier = pltpu.get_barrier_semaphore()

    @pl.loop(1, experts)
    def _(d):
        pl.semaphore_signal(
            barrier, inc=1, device_id={"expert": lax.rem(exp + d, experts)}, device_id_type=MESH_IDS
        )

    for d in (1, mps - 1):
        pl.semaphore_signal(
            barrier, inc=1, device_id={"mp": lax.rem(mp + d, mps)}, device_id_type=MESH_IDS
        )
    for d in (1, segments - 1):
        pl.semaphore_signal(
            barrier, inc=1, device_id={"segment": lax.rem(seg + d, segments)}, device_id_type=MESH_IDS
        )

    w_copies = [
        pltpu.make_async_copy(src, dst, w_sem.at[i])
        for i, (src, dst) in enumerate(((gate_hbm, gate_w), (up_hbm, up_w), (down_hbm, down_w)))
    ]
    for copy in w_copies:
        copy.start()

    row = iota((slots, tok), 0)
    first = routes_ref[0:1, :] == row // per
    second = routes_ref[1:2, :] == row // per
    named = jnp.logical_or(first, second)
    before = (iota((tok, tok), 0) < iota((tok, tok), 1)).astype(bf16)
    earlier = jnp.dot(named.astype(f32).astype(bf16), before, preferred_element_type=f32)
    count[...] = jnp.where(named, earlier, -1.0)
    row_fold = lax.rem(row, per) // SLOTS
    row_slot = lax.rem(row, SLOTS)

    @pl.loop(0, chunks)
    def _(c):
        fill = jnp.where(count[...] == (row_slot + SLOTS * c).astype(f32), 1.0, 0.0)
        picked = jnp.zeros((slots, fold), f32)
        for g in range(FOLDS):
            pick = jnp.where(row_fold == g, fill, 0.0).astype(bf16)
            picked = picked + jnp.dot(
                pick, tokens_ref[:, g * fold : (g + 1) * fold], preferred_element_type=f32
            )
        z_out[c] = picked.astype(bf16)

    pl.semaphore_wait(barrier, experts - 1 + 4)

    def z_go(out, got, send, recv, c):
        base = pl.multiple_of(exp * per, per)
        pltpu.make_async_copy(
            out.at[c, pl.ds(base, per), :], got.at[c, pl.ds(base, per), :], recv.at[c]
        ).start()

        @pl.loop(1, experts)
        def _(d):
            other = lax.rem(exp + d, experts)
            pltpu.make_async_remote_copy(
                src_ref=out.at[c, pl.ds(pl.multiple_of(other * per, per), per), :],
                dst_ref=got.at[c, pl.ds(base, per), :],
                send_sem=send.at[c],
                recv_sem=recv.at[c],
                device_id={"expert": other},
                device_id_type=MESH_IDS,
            ).start()

    def sign(c):
        return 1 - 2 * (c % 2)

    def origin(c, node):
        s = sign(c)
        ox = lax.rem(seg + 2 * segments - s * node[0], segments)
        oy = lax.rem(mp + 2 * mps - s * node[1], mps)
        return ox, oy

    def spot(c, node, half=None):
        ox, oy = origin(c, node)
        r = pl.ds(pl.multiple_of(ox * block, block), block)
        if half is None:
            return r, pl.ds(pl.multiple_of(oy * feat, feat), feat)
        return r, pl.ds(pl.multiple_of(oy * feat + half * half_w, half_w), half_w)

    def hop(c, move):
        s = sign(c)
        if move[0] != 0:
            return {"segment": lax.rem(seg + segments + s * move[0], segments)}
        return {"mp": lax.rem(mp + mps + s * move[1], mps)}

    def send_near(c):
        r, f = spot(c, (0, 0))
        for node in NEAR:
            pltpu.make_async_remote_copy(
                src_ref=rows.at[c, r, f],
                dst_ref=rows.at[c, r, f],
                send_sem=ag_send.at[c],
                recv_sem=ag_recv.at[c, NEAR_ID[node]],
                device_id=hop(c, node),
                device_id_type=MESH_IDS,
            ).start()

    def pass_on(c, half, node):
        for n in children(half, node):
            r, f = spot(c, node, half)
            pltpu.make_async_remote_copy(
                src_ref=rows.at[c, r, f],
                dst_ref=rows.at[c, r, f],
                send_sem=ag_send.at[c],
                recv_sem=ag_recv.at[c, len(NEAR) + FAR_ID[half, n]],
                device_id=hop(c, step_of(node, n)),
                device_id_type=MESH_IDS,
            ).start()

    def wait_far(c, half, node):
        r, f = spot(c, node, half)
        at = rows.at[c, r, f]
        pltpu.make_async_copy(at, at, ag_recv.at[c, len(NEAR) + FAR_ID[half, node]]).wait()

    def from_near(c, node):
        r, f = spot(c, node)
        at = rows.at[c, r, f]
        pltpu.make_async_copy(at, at, ag_recv.at[c, NEAR_ID[node]]).wait()
        pass_on(c, 0, node)
        pass_on(c, 1, node)

    def from_far(c, half, node):
        wait_far(c, half, node)
        pass_on(c, half, node)

    def unfold(c):
        pltpu.make_async_copy(z_in.at[c], z_in.at[c], z_recv.at[c]).wait()
        got = z_in[c]
        r_, q_ = iota((block, slots), 0), iota((block, slots), 1)
        place = (r_ // SLOTS) * per + lax.rem(r_, SLOTS)
        ox = pl.multiple_of(seg * block, block)
        for g in range(FOLDS):
            pick = jnp.where(q_ == place + g * SLOTS, 1.0, 0.0).astype(bf16)
            rows[c, pl.ds(ox, block), pl.ds(pl.multiple_of(mp * feat + g * fold, fold), fold)] = (
                jnp.dot(pick, got, preferred_element_type=f32).astype(bf16)
            )
        send_near(c)

    nt = (((1,), (1,)), ((), ()))

    def fold_gain():
        for copy in w_copies:
            copy.wait()

        @pl.loop(0, feat * mps // 128)
        def _(i):
            cols = pl.ds(pl.multiple_of(i * 128, 128), 128)
            gain = gain_ref[pl.ds(i, 1), :]
            for w in (gate_w, up_w):
                w[:, cols] = (w[:, cols].astype(f32) * gain).astype(bf16)

    def gate_up(c):
        for half, node in FAR:
            if not children(half, node):
                wait_far(c, half, node)
        x = rows[c]
        gate = lax.dot_general(x, gate_w[...], nt, preferred_element_type=f32)
        up = lax.dot_general(x, up_w[...], nt, preferred_element_type=f32)
        squares = jnp.zeros((segments * block, 128), f32)
        for i in range(feat * mps // 128):
            v = rows[c, :, i * 128 : (i + 1) * 128].astype(f32)
            squares = squares + v * v
        mean = jnp.sum(squares, axis=1, keepdims=True) / (feat * mps)
        scale = lax.rsqrt(mean + EPSILON)
        gate = gate * scale
        hidden[c % 2] = (gate / (1.0 + jnp.exp(-gate)) * (up * scale)).astype(bf16)

    def down(c, dy):
        oy = lax.rem(mp + 2 * mps - sign(c) * dy, mps)

        @pl.loop(0, 2)
        def _(i):
            cols = pl.ds(pl.multiple_of(oy * feat + i * half_w, half_w), half_w)
            parts[c, :, cols] = jnp.dot(
                hidden[c % 2], down_w[:, cols], preferred_element_type=f32
            ).astype(bf16)

        for half, node in FAR:
            if node[1] == dy and not children(half, node):
                send_far(c, half, node)

    def add_up(c, half, node):
        below = [FAR_ID[half, n] for n in children(half, node)]
        for i in below:
            at = far_in.at[c, i]
            pltpu.make_async_copy(at, at, rs_recv.at[c, len(NEAR) + i]).wait()
        ox, oy = origin(c, node)
        f = pl.ds(pl.multiple_of(oy * feat + half * half_w, half_w), half_w)

        @pl.loop(0, block // 16)
        def _(k):
            r = pl.ds(pl.multiple_of(ox * block + k * 16, 16), 16)
            acc = parts[c, r, f].astype(f32)
            for i in below:
                acc = acc + far_in[c, i, pl.ds(pl.multiple_of(k * 16, 16), 16), :].astype(f32)
            parts[c, r, f] = acc.astype(bf16)

    def send_far(c, half, node):
        r, f = spot(c, node, half)
        i = FAR_ID[half, node]
        pltpu.make_async_remote_copy(
            src_ref=parts.at[c, r, f],
            dst_ref=far_in.at[c, i],
            send_sem=rs_send.at[c],
            recv_sem=rs_recv.at[c, len(NEAR) + i],
            device_id=hop(c, step_of(node, parent(half, node))),
            device_id_type=MESH_IDS,
        ).start()

    def sum_far(c, half, node):
        add_up(c, half, node)
        send_far(c, half, node)

    def sum_near(c, node):
        for half in (0, 1):
            if children(half, node):
                add_up(c, half, node)
        r, f = spot(c, node)
        pltpu.make_async_remote_copy(
            src_ref=parts.at[c, r, f],
            dst_ref=near_in.at[c, NEAR_ID[node]],
            send_sem=rs_send.at[c],
            recv_sem=rs_recv.at[c, NEAR_ID[node]],
            device_id=hop(c, (-node[0], -node[1])),
            device_id_type=MESH_IDS,
        ).start()

    def finish(c):
        r, _ = spot(c, (0, 0))
        for i in range(len(NEAR)):
            at = near_in.at[c, i]
            pltpu.make_async_copy(at, at, rs_recv.at[c, i]).wait()
        q_, r_ = iota((slots, block), 0), iota((slots, block), 1)
        place = (r_ // SLOTS) * per + lax.rem(r_, SLOTS)
        back = jnp.zeros((slots, fold), f32)
        for g in range(FOLDS):
            acc = parts[c, r, pl.ds(pl.multiple_of(mp * feat + g * fold, fold), fold)].astype(f32)
            for i in range(len(NEAR)):
                acc = acc + near_in[c, i, :, g * fold : (g + 1) * fold].astype(f32)
            pick = jnp.where(q_ == place + g * SLOTS, 1.0, 0.0).astype(bf16)
            back = back + jnp.dot(pick, acc.astype(bf16), preferred_element_type=f32)
        b_out[c] = back.astype(bf16)
        z_go(b_out, b_in, b_send, b_recv, c)

    lane_fold = lax.rem(iota((tok, slots), 1), per) // SLOTS
    lane_slot = lax.rem(iota((tok, slots), 1), SLOTS)

    def combine(c):
        pltpu.make_async_copy(b_in.at[c], b_in.at[c], b_recv.at[c]).wait()
        got = b_in[c]
        share = jnp.where(chosen_n[...] == (lane_slot + SLOTS * c).astype(f32), chosen_w[...], 0.0)
        for g in range(FOLDS):
            part = jnp.where(lane_fold == g, share, 0.0)
            high = part.astype(bf16)
            low = (part - high.astype(f32)).astype(bf16)
            cols = slice(g * fold, (g + 1) * fold)
            total[:, cols] += jnp.dot(high, got, preferred_element_type=f32) + jnp.dot(
                low, got, preferred_element_type=f32
            )

    def weigh():
        total[...] = tokens_ref[...].astype(f32)
        weight = jnp.where(first, gates_ref[0:1, :], 0.0) + jnp.where(second, gates_ref[1:2, :], 0.0)
        chosen_w[...] = jnp.transpose(weight)
        chosen_n[...] = jnp.transpose(count[...])

    steps = {
        "z": lambda c: z_go(z_out, z_in, z_send, z_recv, c),
        "uf": unfold,
        "fn": from_near,
        "ff": from_far,
        "fold": fold_gain,
        "gu": gate_up,
        "dn": down,
        "rf": sum_far,
        "rn": sum_near,
        "fi": finish,
        "co": combine,
    }
    for name, *at in ORDER:
        if name == "fold":
            weigh()
        steps[name](*at)

    out_ref[...] = total[...].astype(bf16)

    sent = segments * mps - 1
    tall = sent * block // mps

    @pl.loop(0, chunks)
    def _(c):
        for ref, sem in ((rows, ag_send), (parts, rs_send)):
            at = ref.at[c, 0:tall, :]
            pltpu.make_async_copy(at, at, sem.at[c]).wait()
        for ref, sem in ((z_out, z_send), (b_out, b_send)):
            at = ref.at[c, 0 : slots - per, :]
            pltpu.make_async_copy(at, at, sem.at[c]).wait()


def body(tokens, routes, gate_weights, norm_gain, gate_proj, up_proj, down_proj):
    experts, segments, mps = (lax.axis_size(a) for a in ("expert", "segment", "mp"))
    tok, feat = tokens.shape[1:]
    capacity = min(tok, 20)
    chunks = -(-capacity // SLOTS)
    fold = feat // FOLDS
    slots = experts * FOLDS * SLOTS
    block = experts * SLOTS
    hid = down_proj.shape[1]
    width = feat * mps
    dims = (experts, segments, mps, tok, feat, chunks)
    bf16, f32 = jnp.bfloat16, jnp.float32
    vmem, dma = pltpu.VMEM, pltpu.SemaphoreType.DMA
    out = pl.pallas_call(
        functools.partial(kernel, dims),
        out_shape=jax.ShapeDtypeStruct((tok, feat), bf16),
        in_specs=[pl.BlockSpec(memory_space=pltpu.VMEM)] * 4 + [pl.BlockSpec(memory_space=pl.ANY)] * 3,
        out_specs=pl.BlockSpec(memory_space=pltpu.VMEM),
        scratch_shapes=[
            vmem((hid, width), bf16),
            vmem((hid, width), bf16),
            vmem((hid, width), bf16),
            vmem((2, segments * block, hid), bf16),
            vmem((chunks, segments * block, width), bf16),
            vmem((chunks, segments * block, width), bf16),
            vmem((chunks, len(FAR), block, feat // 2), bf16),
            vmem((chunks, len(NEAR), block, feat), bf16),
            vmem((chunks, slots, fold), bf16),
            vmem((chunks, slots, fold), bf16),
            vmem((chunks, slots, fold), bf16),
            vmem((chunks, slots, fold), bf16),
            vmem((slots, tok), f32),
            vmem((tok, slots), f32),
            vmem((tok, slots), f32),
            vmem((tok, feat), f32),
            dma((3,)),
            dma((chunks, IDS)),
            dma((chunks, IDS)),
            dma((chunks,)),
            dma((chunks,)),
            dma((chunks,)),
            dma((chunks,)),
            dma((chunks,)),
            dma((chunks,)),
        ],
        compiler_params=pltpu.CompilerParams(
            collective_id=0, has_side_effects=True, vmem_limit_bytes=60 * 1024 * 1024
        ),
        cost_estimate=pl.CostEstimate(
            flops=6 * chunks * segments * block * width * hid,
            bytes_accessed=6 * width * hid,
            transcendentals=chunks * segments * block * hid,
        ),
        name="expert_block",
    )(
        tokens[0],
        jnp.swapaxes(routes, 1, 2)[0],
        jnp.swapaxes(gate_weights, 1, 2)[0],
        norm_gain.reshape(-1, 128),
        jnp.swapaxes(gate_proj, 1, 2)[0],
        jnp.swapaxes(up_proj, 1, 2)[0],
        down_proj[0],
    )
    return out[None]


def solution(mesh):
    placed = (
        P("segment", "expert", "mp"),
        P("segment", "expert", None),
        P("segment", "expert", None),
        P(),
        P("expert", None, ("segment", "mp")),
        P("expert", None, ("segment", "mp")),
        P("expert", ("segment", "mp"), None),
    )
    return jax.shard_map(
        body, mesh=mesh, in_specs=placed, out_specs=P("segment", "expert", "mp"), check_vma=False
    )
```

```python
import functools
import jax
import jax.numpy as jnp
from jax import lax
from jax.experimental import pallas as pl
from jax.experimental.pallas import tpu as pltpu
from jax.sharding import PartitionSpec as P

EPSILON = 1e-06
SLOTS = 4
FOLDS = 4
MESH_IDS = pl.DeviceIdType.MESH

RING = (0, 1, -1, 2)
TURN = {0: -1, 1: 1, -1: -1, 2: 1}


def parent_a(dx, dy):
    if dy in (1, -1):
        return (dx, 0)
    if dy == 2:
        return (dx, TURN[dx])
    return (0, 0) if dx in (1, -1) else (1, 0)


def parent(half, node):
    dx, dy = node
    if half == 0:
        return parent_a(dx, dy)
    py, px = parent_a(dy, dx)
    return (px, py)


def level(node):
    return abs(node[0]) + abs(node[1])


NODES = [(dx, dy) for dx in RING for dy in RING if (dx, dy) != (0, 0)]
NEAR = [n for n in NODES if level(n) == 1]
FAR = [(half, n) for n in NODES if level(n) > 1 for half in (0, 1)]
NEAR_ID = {n: i for i, n in enumerate(NEAR)}
FAR_ID = {m: i for i, m in enumerate(FAR)}
IDS = len(NEAR) + len(FAR)


def children(half, node):
    return [n for h, n in FAR if h == half and parent(half, n) == node]


def depth_below(half, node):
    below = children(half, node)
    return 0 if not below else 1 + max(depth_below(half, n) for n in below)


def step_of(node, up):
    d = (up[0] - node[0], up[1] - node[1])
    return tuple({3: -1, -3: 1}.get(v, v) for v in d)


EARLY = (2, 3, 4)
LATE = (0, 1)
SIDES = [(half, (0, d) if half else (d, 0)) for half in (0, 1) for d in (1, -1, 2)]
SIDE_ID = {m: i for i, m in enumerate(SIDES)}

ORDER = (
    ("mq", 2), ("mq", 3), ("mq", 4), ("z", 0), ("fold",), ("uf", 0), ("z", 1), ("mf", 2), ("z", 2), ("mf", 3),
    ("z", 3), ("mf", 4), ("fn", 0, (0, 1)), ("fn", 0, (0, -1)), ("fn", 0, (1, 0)), ("fn", 0, (-1, 0)), ("z", 4),
    ("uf", 1), ("zx", 2), ("ff", 0, 1, (0, 2)), ("ff", 0, 1, (1, 1)), ("ff", 0, 1, (-1, -1)), ("uf", 2),
    ("ff", 0, 0, (1, 1)), ("ff", 0, 0, (-1, -1)), ("zx", 3), ("ff", 0, 0, (2, 0)), ("uf", 3), ("fn", 1, (0, 1)),
    ("fn", 1, (1, 0)), ("zx", 4), ("fn", 1, (0, -1)), ("fn", 1, (-1, 0)), ("uf", 4), ("fn", 2, (0, 1)),
    ("fn", 2, (0, -1)), ("ff", 0, 1, (1, 2)), ("fn", 2, (-1, 0)), ("ff", 0, 0, (2, 1)), ("fn", 3, (0, 1)),
    ("fn", 2, (1, 0)), ("fn", 3, (1, 0)), ("fn", 3, (0, -1)), ("fn", 3, (-1, 0)), ("ff", 1, 1, (0, 2)),
    ("ff", 1, 1, (1, 1)), ("ff", 1, 0, (1, 1)), ("ff", 1, 0, (2, 0)), ("ff", 1, 1, (-1, -1)), ("ux", 2),
    ("fn", 4, (0, -1)), ("fn", 4, (0, 1)), ("fn", 4, (-1, 0)), ("fn", 4, (1, 0)), ("ff", 1, 0, (-1, -1)),
    ("gu", 0), ("ff", 1, 1, (1, 2)), ("ff", 1, 0, (2, 1)), ("dn", 0, 2), ("dn", 0, 1), ("dn", 0, -1),
    ("dn", 0, 0), ("ff", 2, 0, (1, 1)), ("ff", 2, 1, (1, 1)), ("ff", 2, 0, (-1, -1)), ("ff", 2, 1, (-1, -1)),
    ("rn", 0, (0, 1)), ("ff", 2, 0, (2, 1)), ("rn", 0, (1, 0)), ("ux", 3), ("ff", 2, 1, (1, 2)), ("gu", 1),
    ("rf", 0, 1, (1, 2)), ("rf", 0, 0, (1, 1)), ("rf", 0, 1, (1, 1)), ("rf", 0, 0, (2, 1)),
    ("rf", 0, 0, (-1, -1)), ("rf", 0, 1, (-1, -1)), ("dn", 1, 2), ("dn", 1, 1), ("dn", 1, -1), ("dn", 1, 0),
    ("ff", 3, 0, (1, 1)), ("ff", 3, 1, (1, 1)), ("rn", 0, (0, -1)), ("rn", 0, (-1, 0)), ("rn", 1, (0, 1)),
    ("rn", 1, (1, 0)), ("ux", 4), ("ff", 3, 1, (1, 2)), ("ff", 3, 0, (2, 1)), ("ff", 3, 0, (-1, -1)),
    ("ff", 3, 1, (-1, -1)), ("gu", 2), ("fs", 0), ("rf", 1, 1, (1, 2)), ("rf", 1, 0, (1, 1)),
    ("rf", 1, 1, (1, 1)), ("rf", 1, 0, (2, 1)), ("rf", 1, 0, (-1, -1)), ("rf", 1, 1, (-1, -1)), ("dn", 2, 2),
    ("dn", 2, 1), ("dn", 2, -1), ("dn", 2, 0), ("ff", 4, 0, (1, 1)), ("ff", 4, 1, (1, 1)), ("fi", 0),
    ("ff", 4, 1, (1, 2)), ("ff", 4, 0, (2, 1)), ("ff", 4, 0, (-1, -1)), ("ff", 4, 1, (-1, -1)),
    ("rn", 1, (0, -1)), ("rn", 1, (-1, 0)), ("gu", 3), ("fs", 1), ("rf", 2, 1, (1, 2)), ("rf", 2, 0, (1, 1)),
    ("rf", 2, 1, (1, 1)), ("rf", 2, 0, (2, 1)), ("rf", 2, 0, (-1, -1)), ("rf", 2, 1, (-1, -1)), ("dn", 3, 2),
    ("dn", 3, 1), ("dn", 3, -1), ("rf", 2, 1, (0, 2)), ("dn", 3, 0), ("rf", 2, 0, (2, 0)), ("gu", 4),
    ("rf", 3, 1, (1, 2)), ("rf", 3, 0, (1, 1)), ("rf", 3, 1, (1, 1)), ("rf", 3, 0, (2, 1)),
    ("rf", 3, 0, (-1, -1)), ("rf", 3, 1, (-1, -1)), ("dn", 4, 2), ("dn", 4, 1), ("rf", 3, 1, (0, 2)),
    ("dn", 4, -1), ("dn", 4, 0), ("rf", 3, 0, (2, 0)), ("fi", 1), ("rf", 4, 1, (1, 2)), ("rf", 4, 0, (1, 1)),
    ("rf", 4, 1, (1, 1)), ("rf", 4, 0, (2, 1)), ("rf", 4, 0, (-1, -1)), ("rf", 4, 1, (-1, -1)),
    ("rn", 2, (0, 1)), ("rn", 2, (0, -1)), ("rf", 4, 1, (0, 2)), ("rn", 2, (1, 0)), ("rn", 2, (-1, 0)),
    ("rf", 4, 0, (2, 0)), ("rn", 3, (0, 1)), ("rn", 3, (0, -1)), ("rn", 3, (1, 0)), ("rn", 3, (-1, 0)),
    ("l1", 0), ("rn", 4, (0, -1)), ("rn", 4, (-1, 0)), ("fi", 2), ("rn", 4, (0, 1)), ("rn", 4, (1, 0)),
    ("fi", 3), ("l2", 0), ("l1", 1), ("fi", 4), ("l2", 1), ("co", 0), ("co", 2), ("co", 3), ("co", 1),
    ("co", 4),
)


def kernel(
    dims,
    tokens_ref, routes_ref, gates_ref, gain_ref, gate_hbm, up_hbm, down_hbm,
    out_ref,
    gate_w, up_w, down_w, hidden, rows, parts, far_in, near_in,
    z_out, z_in, b_out, b_in, side, side_in, late_out, late_in, late_near, count, chosen_w, chosen_n, total,
    w_sem, ag_recv, rs_recv, ag_send, rs_send, z_send, z_recv, b_send, b_recv,
    side_send, side_recv, x_send, x_recv, y_send, y_recv, late_send, late_recv,
):
    experts, segments, mps, tok, feat, chunks = dims
    f32, bf16 = jnp.float32, jnp.bfloat16
    fold = feat // FOLDS
    half_w = feat // 2
    part = half_w // FOLDS
    per = FOLDS * SLOTS
    slots = experts * per
    block = experts * SLOTS
    seg, exp, mp = lax.axis_index("segment"), lax.axis_index("expert"), lax.axis_index("mp")

    def iota(shape, dim):
        return lax.broadcasted_iota(jnp.int32, shape, dim)

    barrier = pltpu.get_barrier_semaphore()

    @pl.loop(1, experts)
    def _(d):
        pl.semaphore_signal(
            barrier, inc=1, device_id={"expert": lax.rem(exp + d, experts)}, device_id_type=MESH_IDS
        )

    for d in (1, mps - 1):
        pl.semaphore_signal(
            barrier, inc=1, device_id={"mp": lax.rem(mp + d, mps)}, device_id_type=MESH_IDS
        )
    for d in (1, segments - 1):
        pl.semaphore_signal(
            barrier, inc=1, device_id={"segment": lax.rem(seg + d, segments)}, device_id_type=MESH_IDS
        )

    w_copies = [
        pltpu.make_async_copy(src, dst, w_sem.at[i])
        for i, (src, dst) in enumerate(((gate_hbm, gate_w), (up_hbm, up_w), (down_hbm, down_w)))
    ]
    for copy in w_copies:
        copy.start()

    row = iota((slots, tok), 0)
    first = routes_ref[0:1, :] == row // per
    second = routes_ref[1:2, :] == row // per
    named = jnp.logical_or(first, second)
    before = (iota((tok, tok), 0) < iota((tok, tok), 1)).astype(bf16)
    earlier = jnp.dot(named.astype(f32).astype(bf16), before, preferred_element_type=f32)
    count[...] = jnp.where(named, earlier, -1.0)
    row_fold = lax.rem(row, per) // SLOTS
    row_slot = lax.rem(row, SLOTS)

    @pl.loop(0, chunks)
    def _(c):
        fill = jnp.where(count[...] == (row_slot + SLOTS * c).astype(f32), 1.0, 0.0)
        picked = jnp.zeros((slots, fold), f32)
        for g in range(FOLDS):
            pick = jnp.where(row_fold == g, fill, 0.0).astype(bf16)
            picked = picked + jnp.dot(
                pick,
                jnp.concatenate(
                    [tokens_ref[:, h * half_w + g * part : h * half_w + (g + 1) * part] for h in (0, 1)],
                    axis=1,
                ),
                preferred_element_type=f32,
            )
        z_out[c] = picked.astype(bf16)

    pl.semaphore_wait(barrier, experts - 1 + 4)

    def z_go(out, got, send, recv, c, i=None):
        i = c if i is None else i
        base = pl.multiple_of(exp * per, per)
        pltpu.make_async_copy(
            out.at[i, pl.ds(base, per), :], got.at[i, pl.ds(base, per), :], recv.at[i]
        ).start()

        @pl.loop(1, experts)
        def _(d):
            other = lax.rem(exp + d, experts)
            pltpu.make_async_remote_copy(
                src_ref=out.at[i, pl.ds(pl.multiple_of(other * per, per), per), :],
                dst_ref=got.at[i, pl.ds(base, per), :],
                send_sem=send.at[i],
                recv_sem=recv.at[i],
                device_id={"expert": other},
                device_id_type=MESH_IDS,
            ).start()

    def sign(c):
        return 1 - 2 * (c % 2)

    def origin(c, node):
        s = sign(c)
        ox = lax.rem(seg + 2 * segments - s * node[0], segments)
        oy = lax.rem(mp + 2 * mps - s * node[1], mps)
        return ox, oy

    def spot(c, node, half=None):
        ox, oy = origin(c, node)
        r = pl.ds(pl.multiple_of(ox * block, block), block)
        if half is None:
            return r, pl.ds(pl.multiple_of(oy * feat, feat), feat)
        return r, pl.ds(pl.multiple_of(oy * feat + half * half_w, half_w), half_w)

    def hop(c, move):
        s = sign(c)
        if move[0] != 0:
            return {"segment": lax.rem(seg + segments + s * move[0], segments)}
        return {"mp": lax.rem(mp + mps + s * move[1], mps)}

    def near_half(c, node):
        if c in EARLY:
            return 1 if node[0] else 0
        return None

    def send_near(c):
        for node in NEAR:
            r, f = spot(c, (0, 0), near_half(c, node))
            pltpu.make_async_remote_copy(
                src_ref=rows.at[c, r, f],
                dst_ref=rows.at[c, r, f],
                send_sem=ag_send.at[c],
                recv_sem=ag_recv.at[c, NEAR_ID[node]],
                device_id=hop(c, node),
                device_id_type=MESH_IDS,
            ).start()

    def pass_on(c, half, node):
        for n in children(half, node):
            if c in EARLY and (half, n) in SIDE_ID:
                continue
            r, f = spot(c, node, half)
            pltpu.make_async_remote_copy(
                src_ref=rows.at[c, r, f],
                dst_ref=rows.at[c, r, f],
                send_sem=ag_send.at[c],
                recv_sem=ag_recv.at[c, len(NEAR) + FAR_ID[half, n]],
                device_id=hop(c, step_of(node, n)),
                device_id_type=MESH_IDS,
            ).start()

    def wait_far(c, half, node):
        r, f = spot(c, node, half)
        at = rows.at[c, r, f]
        pltpu.make_async_copy(at, at, ag_recv.at[c, len(NEAR) + FAR_ID[half, node]]).wait()

    def from_near(c, node):
        only = near_half(c, node)
        r, f = spot(c, node, only)
        at = rows.at[c, r, f]
        pltpu.make_async_copy(at, at, ag_recv.at[c, NEAR_ID[node]]).wait()
        for half in (0, 1) if only is None else (only,):
            pass_on(c, half, node)

    def from_far(c, half, node):
        wait_far(c, half, node)
        pass_on(c, half, node)

    def unfold(c):
        pltpu.make_async_copy(z_in.at[c], z_in.at[c], z_recv.at[c]).wait()
        spread(c, z_in[c], [(0, (0, 0)), (1, (0, 0))])
        send_near(c)

    def spread(c, got, places):
        r_, q_ = iota((block, slots), 0), iota((block, slots), 1)
        place = (r_ // SLOTS) * per + lax.rem(r_, SLOTS)
        for g in range(FOLDS):
            pick = jnp.where(q_ == place + g * SLOTS, 1.0, 0.0).astype(bf16)
            whole = jnp.dot(pick, got, preferred_element_type=f32).astype(bf16)
            for i, (half, node) in enumerate(places):
                ox, oy = origin(c, node)
                rows[
                    c,
                    pl.ds(pl.multiple_of(ox * block, block), block),
                    pl.ds(pl.multiple_of(oy * feat + half * half_w + g * part, part), part),
                ] = whole[:, i * part : (i + 1) * part]

    def side_copy(c, half, node, own):
        e, i = EARLY.index(c), SIDE_ID[half, node]
        up = (0, 0) if own else parent(half, node)
        lane = lambda k: pl.ds(k * part, part)
        src = z_out.at[c, :, lane(half)] if own else side.at[e, :, lane(SIDE_ID[half, up])]
        return pltpu.make_async_remote_copy(
            src_ref=src,
            dst_ref=side.at[e, :, lane(i)],
            send_sem=side_send.at[e],
            recv_sem=side_recv.at[e, i],
            device_id=hop(c, step_of(up, node)),
            device_id_type=MESH_IDS,
        )

    def side_wait(c, half, node):
        e, i = EARLY.index(c), SIDE_ID[half, node]
        at = side.at[e, :, pl.ds(i * part, part)]
        pltpu.make_async_copy(at, at, side_recv.at[e, i]).wait()

    def side_first(c):
        for half, node in SIDES:
            if level(node) == 1:
                side_copy(c, half, node, True).start()

    def side_next(c):
        for half, node in SIDES:
            if level(node) == 2:
                side_wait(c, half, parent(half, node))
                side_copy(c, half, node, False).start()

    def side_out(c):
        for half, node in SIDES:
            if level(node) == 2 or node not in [parent(h, n) for h, n in SIDES if h == half]:
                side_wait(c, half, node)
        z_go(side, side_in, x_send, x_recv, c, EARLY.index(c))

    def side_unfold(c):
        e = EARLY.index(c)
        pltpu.make_async_copy(side_in.at[e], side_in.at[e], x_recv.at[e]).wait()
        spread(c, side_in[e], SIDES)
        for half, node in SIDES:
            pass_on(c, half, node)

    nt = (((1,), (1,)), ((), ()))

    def fold_gain():
        for copy in w_copies:
            copy.wait()

        @pl.loop(0, feat * mps // 128)
        def _(i):
            cols = pl.ds(pl.multiple_of(i * 128, 128), 128)
            gain = gain_ref[pl.ds(i, 1), :]
            for w in (gate_w, up_w):
                w[:, cols] = (w[:, cols].astype(f32) * gain).astype(bf16)

    def gate_up(c):
        for half, node in FAR:
            if not children(half, node):
                wait_far(c, half, node)
        x = rows[c]
        gate = lax.dot_general(x, gate_w[...], nt, preferred_element_type=f32)
        up = lax.dot_general(x, up_w[...], nt, preferred_element_type=f32)
        squares = jnp.zeros((segments * block, 128), f32)
        for i in range(feat * mps // 128):
            v = rows[c, :, i * 128 : (i + 1) * 128].astype(f32)
            squares = squares + v * v
        mean = jnp.sum(squares, axis=1, keepdims=True) / (feat * mps)
        scale = lax.rsqrt(mean + EPSILON)
        gate = gate * scale
        hidden[c % 2] = (gate / (1.0 + jnp.exp(-gate)) * (up * scale)).astype(bf16)

    def down(c, dy):
        oy = lax.rem(mp + 2 * mps - sign(c) * dy, mps)

        @pl.loop(0, 2)
        def _(i):
            cols = pl.ds(pl.multiple_of(oy * feat + i * half_w, half_w), half_w)
            parts[c, :, cols] = jnp.dot(
                hidden[c % 2], down_w[:, cols], preferred_element_type=f32
            ).astype(bf16)

        for half, node in FAR:
            if node[1] == dy and not children(half, node):
                send_far(c, half, node)

    def add_up(c, half, node):
        below = [FAR_ID[half, n] for n in children(half, node) if not (c in LATE and (half, n) in SIDE_ID)]
        for i in below:
            at = far_in.at[c, i]
            pltpu.make_async_copy(at, at, rs_recv.at[c, len(NEAR) + i]).wait()
        ox, oy = origin(c, node)
        f = pl.ds(pl.multiple_of(oy * feat + half * half_w, half_w), half_w)

        @pl.loop(0, block // 16)
        def _(k):
            r = pl.ds(pl.multiple_of(ox * block + k * 16, 16), 16)
            acc = parts[c, r, f].astype(f32)
            for i in below:
                acc = acc + far_in[c, i, pl.ds(pl.multiple_of(k * 16, 16), 16), :].astype(f32)
            parts[c, r, f] = acc.astype(bf16)

    def send_far(c, half, node):
        r, f = spot(c, node, half)
        i = FAR_ID[half, node]
        pltpu.make_async_remote_copy(
            src_ref=parts.at[c, r, f],
            dst_ref=far_in.at[c, i],
            send_sem=rs_send.at[c],
            recv_sem=rs_recv.at[c, len(NEAR) + i],
            device_id=hop(c, step_of(node, parent(half, node))),
            device_id_type=MESH_IDS,
        ).start()

    def sum_far(c, half, node):
        add_up(c, half, node)
        send_far(c, half, node)

    def sum_near(c, node):
        only = (1 if node[0] else 0) if c in LATE else None
        for half in (0, 1) if only is None else (only,):
            if children(half, node):
                add_up(c, half, node)
        r, f = spot(c, node, only)
        at = near_in.at[c, NEAR_ID[node]]
        if only is not None:
            at = near_in.at[c, NEAR_ID[node], :, pl.ds(only * half_w, half_w)]
        pltpu.make_async_remote_copy(
            src_ref=parts.at[c, r, f],
            dst_ref=at,
            send_sem=rs_send.at[c],
            recv_sem=rs_recv.at[c, NEAR_ID[node]],
            device_id=hop(c, (-node[0], -node[1])),
            device_id_type=MESH_IDS,
        ).start()

    def gather_up(pieces):
        q_, r_ = iota((slots, block), 0), iota((slots, block), 1)
        place = (r_ // SLOTS) * per + lax.rem(r_, SLOTS)
        back = None
        for g in range(FOLDS):
            pick = jnp.where(q_ == place + g * SLOTS, 1.0, 0.0).astype(bf16)
            add = jnp.dot(pick, pieces(g), preferred_element_type=f32)
            back = add if back is None else back + add
        return back.astype(bf16)

    def finish(c):
        late = c in LATE
        for node in NEAR:
            i = NEAR_ID[node]
            at = near_in.at[c, i]
            if late:
                at = near_in.at[c, i, :, pl.ds((1 if node[0] else 0) * half_w, half_w)]
            pltpu.make_async_copy(at, at, rs_recv.at[c, i]).wait()
        ox = pl.ds(pl.multiple_of(seg * block, block), block)

        def pieces(g):
            both = []
            for half in (0, 1):
                at = half * half_w + g * part
                acc = parts[c, ox, pl.ds(pl.multiple_of(mp * feat + at, part), part)].astype(f32)
                for node in NEAR:
                    if not late or half == (1 if node[0] else 0):
                        acc = acc + near_in[c, NEAR_ID[node], :, at : at + part].astype(f32)
                both.append(acc.astype(bf16))
            return jnp.concatenate(both, axis=1)

        b_out[c] = gather_up(pieces)
        z_go(b_out, b_in, b_send, b_recv, c)

    def finish_side(c):
        e = LATE.index(c)
        for half, node in SIDES:
            add_up(c, half, node)

        def pieces(g):
            whole = []
            for half, node in SIDES:
                ox, oy = origin(c, node)
                whole.append(
                    parts[
                        c,
                        pl.ds(pl.multiple_of(ox * block, block), block),
                        pl.ds(pl.multiple_of(oy * feat + half * half_w + g * part, part), part),
                    ]
                )
            return jnp.concatenate(whole, axis=1)

        late_out[e] = gather_up(pieces)
        z_go(late_out, late_in, y_send, y_recv, c, e)

    def late_copy(c, half, node):
        e, i = LATE.index(c), SIDE_ID[half, node]
        up = parent(half, node)
        return pltpu.make_async_remote_copy(
            src_ref=late_in.at[e, :, pl.ds(i * part, part)],
            dst_ref=late_near.at[e, :, pl.ds(i * part, part)],
            send_sem=late_send.at[e],
            recv_sem=late_recv.at[e, i],
            device_id=hop(c, step_of(node, up)),
            device_id_type=MESH_IDS,
        )

    def late_wait(c, half, node):
        e, i = LATE.index(c), SIDE_ID[half, node]
        at = late_near.at[e, :, pl.ds(i * part, part)]
        pltpu.make_async_copy(at, at, late_recv.at[e, i]).wait()

    def late_first(c):
        e = LATE.index(c)
        pltpu.make_async_copy(late_in.at[e], late_in.at[e], y_recv.at[e]).wait()
        inner = [(h, parent(h, n)) for h, n in SIDES if level(n) == 2]
        for half, node in SIDES:
            if (half, node) not in inner:
                late_copy(c, half, node).start()

    def late_next(c):
        e = LATE.index(c)
        for half, node in SIDES:
            if level(node) == 2:
                late_wait(c, half, node)
                up = parent(half, node)
                f, n = (slice(SIDE_ID[half, v] * part, (SIDE_ID[half, v] + 1) * part) for v in (node, up))
                late_in[e, :, n] = (
                    late_in[e, :, n].astype(f32) + late_near[e, :, f].astype(f32)
                ).astype(bf16)
                late_copy(c, half, up).start()

    lane_fold = lax.rem(iota((tok, slots), 1), per) // SLOTS
    lane_slot = lax.rem(iota((tok, slots), 1), SLOTS)

    def combine(c):
        pltpu.make_async_copy(b_in.at[c], b_in.at[c], b_recv.at[c]).wait()
        got = b_in[c]
        if c in LATE:
            e = LATE.index(c)
            lanes = []
            for half in (0, 1):
                acc = got[:, half * part : (half + 1) * part].astype(f32)
                for h, node in SIDES:
                    if h == half and level(node) == 1:
                        late_wait(c, half, node)
                        i = SIDE_ID[half, node]
                        acc = acc + late_near[e, :, i * part : (i + 1) * part].astype(f32)
                lanes.append(acc.astype(bf16))
            got = jnp.concatenate(lanes, axis=1)
        share = jnp.where(chosen_n[...] == (lane_slot + SLOTS * c).astype(f32), chosen_w[...], 0.0)
        for g in range(FOLDS):
            mine = jnp.where(lane_fold == g, share, 0.0)
            high = mine.astype(bf16)
            low = (mine - high.astype(f32)).astype(bf16)
            add = jnp.dot(high, got, preferred_element_type=f32) + jnp.dot(
                low, got, preferred_element_type=f32
            )
            for half in (0, 1):
                at = half * half_w + g * part
                total[:, at : at + part] += add[:, half * part : (half + 1) * part]

    def weigh():
        total[...] = tokens_ref[...].astype(f32)
        weight = jnp.where(first, gates_ref[0:1, :], 0.0) + jnp.where(second, gates_ref[1:2, :], 0.0)
        chosen_w[...] = jnp.transpose(weight)
        chosen_n[...] = jnp.transpose(count[...])

    steps = {
        "z": lambda c: z_go(z_out, z_in, z_send, z_recv, c),
        "mq": side_first,
        "mf": side_next,
        "zx": side_out,
        "uf": unfold,
        "ux": side_unfold,
        "fn": from_near,
        "ff": from_far,
        "fold": fold_gain,
        "gu": gate_up,
        "dn": down,
        "rf": sum_far,
        "rn": sum_near,
        "fi": finish,
        "fs": finish_side,
        "l1": late_first,
        "l2": late_next,
        "co": combine,
    }
    for name, *at in ORDER:
        if name == "fold":
            weigh()
        steps[name](*at)

    out_ref[...] = total[...].astype(bf16)

    def blocks(chunk_list, count, ref, sem):
        for c in chunk_list:
            at = ref.at[c, 0 : count * block // (2 * mps), :]
            pltpu.make_async_copy(at, at, sem.at[c]).wait()

    whole = 2 * (segments * mps - 1)
    short = len(SIDES)
    blocks([c for c in range(chunks) if c not in EARLY], whole, rows, ag_send)
    blocks(EARLY, whole - short, rows, ag_send)
    blocks([c for c in range(chunks) if c not in LATE], whole, parts, rs_send)
    blocks(LATE, whole - short, parts, rs_send)
    for ref, sem, n in (
        (z_out, z_send, chunks),
        (b_out, b_send, chunks),
        (side, x_send, len(EARLY)),
        (late_out, y_send, len(LATE)),
    ):
        for c in range(n):
            at = ref.at[c, 0 : slots - per, :]
            pltpu.make_async_copy(at, at, sem.at[c]).wait()
    for ref, sem, n in ((side, side_send, len(EARLY)), (late_in, late_send, len(LATE))):
        for c in range(n):
            pltpu.make_async_copy(ref.at[c], ref.at[c], sem.at[c]).wait()


def body(tokens, routes, gate_weights, norm_gain, gate_proj, up_proj, down_proj):
    experts, segments, mps = (lax.axis_size(a) for a in ("expert", "segment", "mp"))
    tok, feat = tokens.shape[1:]
    capacity = min(tok, 20)
    chunks = -(-capacity // SLOTS)
    fold = feat // FOLDS
    slots = experts * FOLDS * SLOTS
    block = experts * SLOTS
    hid = down_proj.shape[1]
    width = feat * mps
    dims = (experts, segments, mps, tok, feat, chunks)
    bf16, f32 = jnp.bfloat16, jnp.float32
    early, late = max(len(EARLY), 1), max(len(LATE), 1)
    vmem, dma = pltpu.VMEM, pltpu.SemaphoreType.DMA
    out = pl.pallas_call(
        functools.partial(kernel, dims),
        out_shape=jax.ShapeDtypeStruct((tok, feat), bf16),
        in_specs=[pl.BlockSpec(memory_space=pltpu.VMEM)] * 4 + [pl.BlockSpec(memory_space=pl.ANY)] * 3,
        out_specs=pl.BlockSpec(memory_space=pltpu.VMEM),
        scratch_shapes=[
            vmem((hid, width), bf16),
            vmem((hid, width), bf16),
            vmem((hid, width), bf16),
            vmem((2, segments * block, hid), bf16),
            vmem((chunks, segments * block, width), bf16),
            vmem((chunks, segments * block, width), bf16),
            vmem((chunks, len(FAR), block, feat // 2), bf16),
            vmem((chunks, len(NEAR), block, feat), bf16),
            vmem((chunks, slots, fold), bf16),
            vmem((chunks, slots, fold), bf16),
            vmem((chunks, slots, fold), bf16),
            vmem((chunks, slots, fold), bf16),
            vmem((early, slots, len(SIDES) * fold // 2), bf16),
            vmem((early, slots, len(SIDES) * fold // 2), bf16),
            vmem((late, slots, len(SIDES) * fold // 2), bf16),
            vmem((late, slots, len(SIDES) * fold // 2), bf16),
            vmem((late, slots, len(SIDES) * fold // 2), bf16),
            vmem((slots, tok), f32),
            vmem((tok, slots), f32),
            vmem((tok, slots), f32),
            vmem((tok, feat), f32),
            dma((3,)),
            dma((chunks, IDS)),
            dma((chunks, IDS)),
            dma((chunks,)),
            dma((chunks,)),
            dma((chunks,)),
            dma((chunks,)),
            dma((chunks,)),
            dma((chunks,)),
            dma((early,)),
            dma((early, len(SIDES))),
            dma((early,)),
            dma((early,)),
            dma((late,)),
            dma((late,)),
            dma((late,)),
            dma((late, len(SIDES))),
        ],
        compiler_params=pltpu.CompilerParams(
            collective_id=0, has_side_effects=True, vmem_limit_bytes=60 * 1024 * 1024
        ),
        cost_estimate=pl.CostEstimate(
            flops=6 * chunks * segments * block * width * hid,
            bytes_accessed=6 * width * hid,
            transcendentals=chunks * segments * block * hid,
        ),
        name="expert_block",
    )(
        tokens[0],
        jnp.swapaxes(routes, 1, 2)[0],
        jnp.swapaxes(gate_weights, 1, 2)[0],
        norm_gain.reshape(-1, 128),
        jnp.swapaxes(gate_proj, 1, 2)[0],
        jnp.swapaxes(up_proj, 1, 2)[0],
        down_proj[0],
    )
    return out[None]


def solution(mesh):
    placed = (
        P("segment", "expert", "mp"),
        P("segment", "expert", None),
        P("segment", "expert", None),
        P(),
        P("expert", None, ("segment", "mp")),
        P("expert", None, ("segment", "mp")),
        P("expert", ("segment", "mp"), None),
    )
    return jax.shard_map(
        body, mesh=mesh, in_specs=placed, out_specs=P("segment", "expert", "mp"), check_vma=False
    )
```

```python
import functools
import jax
import jax.numpy as jnp
from jax import lax
from jax.experimental import pallas as pl
from jax.experimental.pallas import tpu as pltpu
from jax.sharding import PartitionSpec as P

EPSILON = 1e-06
SLOTS = 4
FOLDS = 4
MESH_IDS = pl.DeviceIdType.MESH

RING = (0, 1, -1, 2)
TURN = {0: -1, 1: 1, -1: -1, 2: 1}


def parent_a(dx, dy):
    if dy in (1, -1):
        return (dx, 0)
    if dy == 2:
        return (dx, TURN[dx])
    return (0, 0) if dx in (1, -1) else (1, 0)


def parent(half, node):
    dx, dy = node
    if half == 0:
        return parent_a(dx, dy)
    py, px = parent_a(dy, dx)
    return (px, py)


def level(node):
    return abs(node[0]) + abs(node[1])


NODES = [(dx, dy) for dx in RING for dy in RING if (dx, dy) != (0, 0)]
NEAR = [n for n in NODES if level(n) == 1]
FAR = [(half, n) for n in NODES if level(n) > 1 for half in (0, 1)]
NEAR_ID = {n: i for i, n in enumerate(NEAR)}
FAR_ID = {m: i for i, m in enumerate(FAR)}
IDS = len(NEAR) + len(FAR)


def children(half, node):
    return [n for h, n in FAR if h == half and parent(half, n) == node]


def depth_below(half, node):
    below = children(half, node)
    return 0 if not below else 1 + max(depth_below(half, n) for n in below)


def step_of(node, up):
    d = (up[0] - node[0], up[1] - node[1])
    return tuple({3: -1, -3: 1}.get(v, v) for v in d)


EARLY = (2, 3, 4)
LATE = (0, 1, 2)
SIDES = [(half, (0, d) if half else (d, 0)) for half in (0, 1) for d in (1, -1, 2)]
SIDE_ID = {m: i for i, m in enumerate(SIDES)}

ORDER = (
    ("mq", 2), ("mq", 3), ("mq", 4), ("z", 0), ("fold",), ("mf", 2), ("uf", 0), ("mf", 3), ("mf", 4), ("z", 1),
    ("z", 2), ("z", 3), ("fn", 0, (0, -1)), ("fn", 0, (-1, 0)), ("fn", 0, (1, 0)), ("fn", 0, (0, 1)), ("z", 4),
    ("zx", 2), ("ff", 0, 1, (-1, -1)), ("uf", 1), ("ff", 0, 0, (-1, -1)), ("ff", 0, 0, (2, 0)),
    ("ff", 0, 0, (1, 1)), ("uf", 2), ("ff", 0, 1, (1, 1)), ("ff", 0, 1, (0, 2)), ("zx", 3), ("zx", 4),
    ("fn", 1, (0, 1)), ("fn", 1, (-1, 0)), ("fn", 1, (0, -1)), ("uf", 3), ("ff", 0, 0, (2, 1)),
    ("fn", 1, (1, 0)), ("fn", 2, (1, 0)), ("uf", 4), ("fn", 2, (-1, 0)), ("fn", 2, (0, -1)),
    ("ff", 0, 1, (1, 2)), ("fn", 2, (0, 1)), ("ff", 1, 1, (0, 2)), ("ff", 1, 1, (1, 1)), ("ff", 1, 0, (-1, -1)),
    ("fn", 3, (0, 1)), ("fn", 3, (1, 0)), ("ff", 1, 1, (-1, -1)), ("fn", 3, (0, -1)), ("ff", 1, 0, (1, 1)),
    ("ff", 1, 0, (2, 0)), ("fn", 3, (-1, 0)), ("ux", 2), ("fn", 4, (0, -1)), ("gu", 0), ("ff", 1, 1, (1, 2)),
    ("ff", 1, 0, (2, 1)), ("dn", 0, 2), ("dn", 0, 1), ("dn", 0, -1), ("dn", 0, 0), ("ff", 2, 0, (1, 1)),
    ("ff", 2, 1, (1, 1)), ("ff", 2, 0, (-1, -1)), ("ff", 2, 1, (-1, -1)), ("rn", 0, (0, 1)), ("rn", 0, (1, 0)),
    ("fn", 4, (0, 1)), ("fn", 4, (1, 0)), ("fn", 4, (-1, 0)), ("ux", 3), ("ff", 2, 1, (1, 2)),
    ("ff", 2, 0, (2, 1)), ("rf", 0, 1, (1, 2)), ("gu", 1), ("rf", 0, 0, (1, 1)), ("rf", 0, 1, (1, 1)),
    ("rf", 0, 0, (2, 1)), ("rf", 0, 0, (-1, -1)), ("rf", 0, 1, (-1, -1)), ("dn", 1, 2), ("dn", 1, 1),
    ("dn", 1, -1), ("dn", 1, 0), ("ff", 3, 0, (1, 1)), ("ff", 3, 1, (1, 1)), ("rn", 0, (0, -1)),
    ("rn", 0, (-1, 0)), ("ff", 3, 0, (-1, -1)), ("ff", 3, 1, (-1, -1)), ("rn", 1, (0, 1)), ("rn", 1, (1, 0)),
    ("ux", 4), ("ff", 3, 1, (1, 2)), ("ff", 3, 0, (2, 1)), ("gu", 2), ("rf", 1, 1, (1, 2)),
    ("rf", 1, 0, (1, 1)), ("rf", 1, 1, (1, 1)), ("rf", 1, 0, (2, 1)), ("rf", 1, 0, (-1, -1)), ("dn", 2, 2),
    ("dn", 2, 1), ("rf", 1, 1, (-1, -1)), ("dn", 2, -1), ("dn", 2, 0), ("fs", 0), ("rn", 1, (0, -1)),
    ("ff", 4, 1, (1, 1)), ("ff", 4, 0, (1, 1)), ("rn", 1, (-1, 0)), ("rn", 2, (0, 1)), ("rn", 2, (1, 0)),
    ("fi", 0), ("ff", 4, 1, (1, 2)), ("ff", 4, 0, (2, 1)), ("ff", 4, 0, (-1, -1)), ("ff", 4, 1, (-1, -1)),
    ("gu", 3), ("rf", 2, 1, (1, 2)), ("rf", 2, 0, (1, 1)), ("rf", 2, 1, (1, 1)), ("rf", 2, 0, (2, 1)),
    ("dn", 3, 2), ("rf", 2, 0, (-1, -1)), ("dn", 3, 1), ("rf", 2, 1, (-1, -1)), ("dn", 3, -1), ("dn", 3, 0),
    ("fs", 1), ("gu", 4), ("rf", 3, 1, (1, 2)), ("rf", 3, 0, (1, 1)), ("rf", 3, 1, (1, 1)),
    ("rf", 3, 0, (2, 1)), ("rf", 3, 0, (-1, -1)), ("dn", 4, 2), ("dn", 4, 1), ("rf", 3, 1, (-1, -1)),
    ("dn", 4, -1), ("dn", 4, 0), ("fs", 2), ("rf", 4, 1, (1, 2)), ("rf", 4, 0, (1, 1)), ("rf", 4, 1, (1, 1)),
    ("rf", 4, 0, (-1, -1)), ("rf", 4, 0, (2, 1)), ("rf", 3, 1, (0, 2)), ("rf", 4, 1, (-1, -1)),
    ("rf", 3, 0, (2, 0)), ("rn", 2, (0, -1)), ("rn", 2, (-1, 0)), ("rn", 3, (0, -1)), ("rn", 3, (-1, 0)),
    ("rf", 4, 1, (0, 2)), ("fi", 1), ("rf", 4, 0, (2, 0)), ("rn", 3, (0, 1)), ("rn", 3, (1, 0)), ("l1", 0),
    ("rn", 4, (0, -1)), ("rn", 4, (-1, 0)), ("rn", 4, (0, 1)), ("rn", 4, (1, 0)), ("fi", 2), ("l1", 1),
    ("fi", 3), ("l1", 2), ("l2", 0), ("fi", 4), ("l2", 1), ("l2", 2), ("co", 0), ("co", 3), ("co", 1),
    ("co", 2), ("co", 4),
)


def kernel(
    dims,
    tokens_ref, routes_ref, gates_ref, gain_ref, gate_hbm, up_hbm, down_hbm,
    out_ref,
    gate_w, up_w, down_w, hidden, rows, parts, far_in, near_in,
    z_out, z_in, b_out, b_in, side, side_in, late_out, late_in, late_near, count, chosen_w, chosen_n, total,
    w_sem, ag_recv, rs_recv, ag_send, rs_send, z_send, z_recv, b_send, b_recv,
    side_send, side_recv, x_send, x_recv, y_send, y_recv, late_send, late_recv,
):
    experts, segments, mps, tok, feat, chunks = dims
    f32, bf16 = jnp.float32, jnp.bfloat16
    fold = feat // FOLDS
    half_w = feat // 2
    part = half_w // FOLDS
    per = FOLDS * SLOTS
    slots = experts * per
    block = experts * SLOTS
    seg, exp, mp = lax.axis_index("segment"), lax.axis_index("expert"), lax.axis_index("mp")

    def iota(shape, dim):
        return lax.broadcasted_iota(jnp.int32, shape, dim)

    barrier = pltpu.get_barrier_semaphore()

    @pl.loop(1, experts)
    def _(d):
        pl.semaphore_signal(
            barrier, inc=1, device_id={"expert": lax.rem(exp + d, experts)}, device_id_type=MESH_IDS
        )

    for d in (1, mps - 1):
        pl.semaphore_signal(
            barrier, inc=1, device_id={"mp": lax.rem(mp + d, mps)}, device_id_type=MESH_IDS
        )
    for d in (1, segments - 1):
        pl.semaphore_signal(
            barrier, inc=1, device_id={"segment": lax.rem(seg + d, segments)}, device_id_type=MESH_IDS
        )

    w_copies = [
        pltpu.make_async_copy(src, dst, w_sem.at[i])
        for i, (src, dst) in enumerate(((gate_hbm, gate_w), (up_hbm, up_w), (down_hbm, down_w)))
    ]
    for copy in w_copies:
        copy.start()

    row = iota((slots, tok), 0)
    first = routes_ref[0:1, :] == row // per
    second = routes_ref[1:2, :] == row // per
    named = jnp.logical_or(first, second)
    before = (iota((tok, tok), 0) < iota((tok, tok), 1)).astype(bf16)
    earlier = jnp.dot(named.astype(f32).astype(bf16), before, preferred_element_type=f32)
    count[...] = jnp.where(named, earlier, -1.0)
    row_fold = lax.rem(row, per) // SLOTS
    row_slot = lax.rem(row, SLOTS)

    @pl.loop(0, chunks)
    def _(c):
        fill = jnp.where(count[...] == (row_slot + SLOTS * c).astype(f32), 1.0, 0.0)
        picked = jnp.zeros((slots, fold), f32)
        for g in range(FOLDS):
            pick = jnp.where(row_fold == g, fill, 0.0).astype(bf16)
            picked = picked + jnp.dot(
                pick,
                jnp.concatenate(
                    [tokens_ref[:, h * half_w + g * part : h * half_w + (g + 1) * part] for h in (0, 1)],
                    axis=1,
                ),
                preferred_element_type=f32,
            )
        z_out[c] = picked.astype(bf16)

    pl.semaphore_wait(barrier, experts - 1 + 4)

    def z_go(out, got, send, recv, c, i=None):
        i = c if i is None else i
        base = pl.multiple_of(exp * per, per)
        pltpu.make_async_copy(
            out.at[i, pl.ds(base, per), :], got.at[i, pl.ds(base, per), :], recv.at[i]
        ).start()

        @pl.loop(1, experts)
        def _(d):
            other = lax.rem(exp + d, experts)
            pltpu.make_async_remote_copy(
                src_ref=out.at[i, pl.ds(pl.multiple_of(other * per, per), per), :],
                dst_ref=got.at[i, pl.ds(base, per), :],
                send_sem=send.at[i],
                recv_sem=recv.at[i],
                device_id={"expert": other},
                device_id_type=MESH_IDS,
            ).start()

    def sign(c):
        return 1 - 2 * (c % 2)

    def origin(c, node):
        s = sign(c)
        ox = lax.rem(seg + 2 * segments - s * node[0], segments)
        oy = lax.rem(mp + 2 * mps - s * node[1], mps)
        return ox, oy

    def spot(c, node, half=None):
        ox, oy = origin(c, node)
        r = pl.ds(pl.multiple_of(ox * block, block), block)
        if half is None:
            return r, pl.ds(pl.multiple_of(oy * feat, feat), feat)
        return r, pl.ds(pl.multiple_of(oy * feat + half * half_w, half_w), half_w)

    def hop(c, move):
        s = sign(c)
        if move[0] != 0:
            return {"segment": lax.rem(seg + segments + s * move[0], segments)}
        return {"mp": lax.rem(mp + mps + s * move[1], mps)}

    def near_half(c, node):
        if c in EARLY:
            return 1 if node[0] else 0
        return None

    def send_near(c):
        for node in NEAR:
            r, f = spot(c, (0, 0), near_half(c, node))
            pltpu.make_async_remote_copy(
                src_ref=rows.at[c, r, f],
                dst_ref=rows.at[c, r, f],
                send_sem=ag_send.at[c],
                recv_sem=ag_recv.at[c, NEAR_ID[node]],
                device_id=hop(c, node),
                device_id_type=MESH_IDS,
            ).start()

    def pass_on(c, half, node):
        for n in children(half, node):
            if c in EARLY and (half, n) in SIDE_ID:
                continue
            r, f = spot(c, node, half)
            pltpu.make_async_remote_copy(
                src_ref=rows.at[c, r, f],
                dst_ref=rows.at[c, r, f],
                send_sem=ag_send.at[c],
                recv_sem=ag_recv.at[c, len(NEAR) + FAR_ID[half, n]],
                device_id=hop(c, step_of(node, n)),
                device_id_type=MESH_IDS,
            ).start()

    def wait_far(c, half, node):
        r, f = spot(c, node, half)
        at = rows.at[c, r, f]
        pltpu.make_async_copy(at, at, ag_recv.at[c, len(NEAR) + FAR_ID[half, node]]).wait()

    def from_near(c, node):
        only = near_half(c, node)
        r, f = spot(c, node, only)
        at = rows.at[c, r, f]
        pltpu.make_async_copy(at, at, ag_recv.at[c, NEAR_ID[node]]).wait()
        for half in (0, 1) if only is None else (only,):
            pass_on(c, half, node)

    def from_far(c, half, node):
        wait_far(c, half, node)
        pass_on(c, half, node)

    def unfold(c):
        pltpu.make_async_copy(z_in.at[c], z_in.at[c], z_recv.at[c]).wait()
        spread(c, z_in[c], [(0, (0, 0)), (1, (0, 0))])
        send_near(c)

    def spread(c, got, places):
        r_, q_ = iota((block, slots), 0), iota((block, slots), 1)
        place = (r_ // SLOTS) * per + lax.rem(r_, SLOTS)
        for g in range(FOLDS):
            pick = jnp.where(q_ == place + g * SLOTS, 1.0, 0.0).astype(bf16)
            whole = jnp.dot(pick, got, preferred_element_type=f32).astype(bf16)
            for i, (half, node) in enumerate(places):
                ox, oy = origin(c, node)
                rows[
                    c,
                    pl.ds(pl.multiple_of(ox * block, block), block),
                    pl.ds(pl.multiple_of(oy * feat + half * half_w + g * part, part), part),
                ] = whole[:, i * part : (i + 1) * part]

    def side_copy(c, half, node, own):
        e, i = EARLY.index(c), SIDE_ID[half, node]
        up = (0, 0) if own else parent(half, node)
        lane = lambda k: pl.ds(k * part, part)
        src = z_out.at[c, :, lane(half)] if own else side.at[e, :, lane(SIDE_ID[half, up])]
        return pltpu.make_async_remote_copy(
            src_ref=src,
            dst_ref=side.at[e, :, lane(i)],
            send_sem=side_send.at[e],
            recv_sem=side_recv.at[e, i],
            device_id=hop(c, step_of(up, node)),
            device_id_type=MESH_IDS,
        )

    def side_wait(c, half, node):
        e, i = EARLY.index(c), SIDE_ID[half, node]
        at = side.at[e, :, pl.ds(i * part, part)]
        pltpu.make_async_copy(at, at, side_recv.at[e, i]).wait()

    def side_first(c):
        for half, node in SIDES:
            if level(node) == 1:
                side_copy(c, half, node, True).start()

    def side_next(c):
        for half, node in SIDES:
            if level(node) == 2:
                side_wait(c, half, parent(half, node))
                side_copy(c, half, node, False).start()

    def side_out(c):
        for half, node in SIDES:
            if level(node) == 2 or node not in [parent(h, n) for h, n in SIDES if h == half]:
                side_wait(c, half, node)
        z_go(side, side_in, x_send, x_recv, c, EARLY.index(c))

    def side_unfold(c):
        e = EARLY.index(c)
        pltpu.make_async_copy(side_in.at[e], side_in.at[e], x_recv.at[e]).wait()
        spread(c, side_in[e], SIDES)
        for half, node in SIDES:
            pass_on(c, half, node)

    nt = (((1,), (1,)), ((), ()))

    def fold_gain():
        for copy in w_copies:
            copy.wait()

        @pl.loop(0, feat * mps // 128)
        def _(i):
            cols = pl.ds(pl.multiple_of(i * 128, 128), 128)
            gain = gain_ref[pl.ds(i, 1), :]
            for w in (gate_w, up_w):
                w[:, cols] = (w[:, cols].astype(f32) * gain).astype(bf16)

    def gate_up(c):
        for half, node in FAR:
            if not children(half, node):
                wait_far(c, half, node)
        x = rows[c]
        gate = lax.dot_general(x, gate_w[...], nt, preferred_element_type=f32)
        up = lax.dot_general(x, up_w[...], nt, preferred_element_type=f32)
        squares = jnp.zeros((segments * block, 128), f32)
        for i in range(feat * mps // 128):
            v = rows[c, :, i * 128 : (i + 1) * 128].astype(f32)
            squares = squares + v * v
        mean = jnp.sum(squares, axis=1, keepdims=True) / (feat * mps)
        scale = lax.rsqrt(mean + EPSILON)
        gate = gate * scale
        hidden[c % 2] = (gate / (1.0 + jnp.exp(-gate)) * (up * scale)).astype(bf16)

    def down(c, dy):
        oy = lax.rem(mp + 2 * mps - sign(c) * dy, mps)

        @pl.loop(0, 2)
        def _(i):
            cols = pl.ds(pl.multiple_of(oy * feat + i * half_w, half_w), half_w)
            parts[c, :, cols] = jnp.dot(
                hidden[c % 2], down_w[:, cols], preferred_element_type=f32
            ).astype(bf16)

        for half, node in FAR:
            if node[1] == dy and not children(half, node):
                send_far(c, half, node)

    def add_up(c, half, node):
        below = [FAR_ID[half, n] for n in children(half, node) if not (c in LATE and (half, n) in SIDE_ID)]
        for i in below:
            at = far_in.at[c, i]
            pltpu.make_async_copy(at, at, rs_recv.at[c, len(NEAR) + i]).wait()
        ox, oy = origin(c, node)
        f = pl.ds(pl.multiple_of(oy * feat + half * half_w, half_w), half_w)

        @pl.loop(0, block // 16)
        def _(k):
            r = pl.ds(pl.multiple_of(ox * block + k * 16, 16), 16)
            acc = parts[c, r, f].astype(f32)
            for i in below:
                acc = acc + far_in[c, i, pl.ds(pl.multiple_of(k * 16, 16), 16), :].astype(f32)
            parts[c, r, f] = acc.astype(bf16)

    def send_far(c, half, node):
        r, f = spot(c, node, half)
        i = FAR_ID[half, node]
        pltpu.make_async_remote_copy(
            src_ref=parts.at[c, r, f],
            dst_ref=far_in.at[c, i],
            send_sem=rs_send.at[c],
            recv_sem=rs_recv.at[c, len(NEAR) + i],
            device_id=hop(c, step_of(node, parent(half, node))),
            device_id_type=MESH_IDS,
        ).start()

    def sum_far(c, half, node):
        add_up(c, half, node)
        send_far(c, half, node)

    def sum_near(c, node):
        only = (1 if node[0] else 0) if c in LATE else None
        for half in (0, 1) if only is None else (only,):
            if children(half, node):
                add_up(c, half, node)
        r, f = spot(c, node, only)
        at = near_in.at[c, NEAR_ID[node]]
        if only is not None:
            at = near_in.at[c, NEAR_ID[node], :, pl.ds(only * half_w, half_w)]
        pltpu.make_async_remote_copy(
            src_ref=parts.at[c, r, f],
            dst_ref=at,
            send_sem=rs_send.at[c],
            recv_sem=rs_recv.at[c, NEAR_ID[node]],
            device_id=hop(c, (-node[0], -node[1])),
            device_id_type=MESH_IDS,
        ).start()

    def gather_up(pieces):
        q_, r_ = iota((slots, block), 0), iota((slots, block), 1)
        place = (r_ // SLOTS) * per + lax.rem(r_, SLOTS)
        back = None
        for g in range(FOLDS):
            pick = jnp.where(q_ == place + g * SLOTS, 1.0, 0.0).astype(bf16)
            add = jnp.dot(pick, pieces(g), preferred_element_type=f32)
            back = add if back is None else back + add
        return back.astype(bf16)

    def finish(c):
        late = c in LATE
        for node in NEAR:
            i = NEAR_ID[node]
            at = near_in.at[c, i]
            if late:
                at = near_in.at[c, i, :, pl.ds((1 if node[0] else 0) * half_w, half_w)]
            pltpu.make_async_copy(at, at, rs_recv.at[c, i]).wait()
        ox = pl.ds(pl.multiple_of(seg * block, block), block)

        def pieces(g):
            both = []
            for half in (0, 1):
                at = half * half_w + g * part
                acc = parts[c, ox, pl.ds(pl.multiple_of(mp * feat + at, part), part)].astype(f32)
                for node in NEAR:
                    if not late or half == (1 if node[0] else 0):
                        acc = acc + near_in[c, NEAR_ID[node], :, at : at + part].astype(f32)
                both.append(acc.astype(bf16))
            return jnp.concatenate(both, axis=1)

        b_out[c] = gather_up(pieces)
        z_go(b_out, b_in, b_send, b_recv, c)

    def finish_side(c):
        e = LATE.index(c)
        for half, node in SIDES:
            add_up(c, half, node)

        def pieces(g):
            whole = []
            for half, node in SIDES:
                ox, oy = origin(c, node)
                whole.append(
                    parts[
                        c,
                        pl.ds(pl.multiple_of(ox * block, block), block),
                        pl.ds(pl.multiple_of(oy * feat + half * half_w + g * part, part), part),
                    ]
                )
            return jnp.concatenate(whole, axis=1)

        late_out[e] = gather_up(pieces)
        z_go(late_out, late_in, y_send, y_recv, c, e)

    def late_copy(c, half, node):
        e, i = LATE.index(c), SIDE_ID[half, node]
        up = parent(half, node)
        return pltpu.make_async_remote_copy(
            src_ref=late_in.at[e, :, pl.ds(i * part, part)],
            dst_ref=late_near.at[e, :, pl.ds(i * part, part)],
            send_sem=late_send.at[e],
            recv_sem=late_recv.at[e, i],
            device_id=hop(c, step_of(node, up)),
            device_id_type=MESH_IDS,
        )

    def late_wait(c, half, node):
        e, i = LATE.index(c), SIDE_ID[half, node]
        at = late_near.at[e, :, pl.ds(i * part, part)]
        pltpu.make_async_copy(at, at, late_recv.at[e, i]).wait()

    def late_first(c):
        e = LATE.index(c)
        pltpu.make_async_copy(late_in.at[e], late_in.at[e], y_recv.at[e]).wait()
        inner = [(h, parent(h, n)) for h, n in SIDES if level(n) == 2]
        for half, node in SIDES:
            if (half, node) not in inner:
                late_copy(c, half, node).start()

    def late_next(c):
        e = LATE.index(c)
        for half, node in SIDES:
            if level(node) == 2:
                late_wait(c, half, node)
                up = parent(half, node)
                f, n = (slice(SIDE_ID[half, v] * part, (SIDE_ID[half, v] + 1) * part) for v in (node, up))
                late_in[e, :, n] = (
                    late_in[e, :, n].astype(f32) + late_near[e, :, f].astype(f32)
                ).astype(bf16)
                late_copy(c, half, up).start()

    lane_fold = lax.rem(iota((tok, slots), 1), per) // SLOTS
    lane_slot = lax.rem(iota((tok, slots), 1), SLOTS)

    def combine(c):
        pltpu.make_async_copy(b_in.at[c], b_in.at[c], b_recv.at[c]).wait()
        got = b_in[c]
        if c in LATE:
            e = LATE.index(c)
            lanes = []
            for half in (0, 1):
                acc = got[:, half * part : (half + 1) * part].astype(f32)
                for h, node in SIDES:
                    if h == half and level(node) == 1:
                        late_wait(c, half, node)
                        i = SIDE_ID[half, node]
                        acc = acc + late_near[e, :, i * part : (i + 1) * part].astype(f32)
                lanes.append(acc.astype(bf16))
            got = jnp.concatenate(lanes, axis=1)
        share = jnp.where(chosen_n[...] == (lane_slot + SLOTS * c).astype(f32), chosen_w[...], 0.0)
        for g in range(FOLDS):
            mine = jnp.where(lane_fold == g, share, 0.0)
            high = mine.astype(bf16)
            low = (mine - high.astype(f32)).astype(bf16)
            add = jnp.dot(high, got, preferred_element_type=f32) + jnp.dot(
                low, got, preferred_element_type=f32
            )
            for half in (0, 1):
                at = half * half_w + g * part
                total[:, at : at + part] += add[:, half * part : (half + 1) * part]

    def weigh():
        total[...] = tokens_ref[...].astype(f32)
        weight = jnp.where(first, gates_ref[0:1, :], 0.0) + jnp.where(second, gates_ref[1:2, :], 0.0)
        chosen_w[...] = jnp.transpose(weight)
        chosen_n[...] = jnp.transpose(count[...])

    steps = {
        "z": lambda c: z_go(z_out, z_in, z_send, z_recv, c),
        "mq": side_first,
        "mf": side_next,
        "zx": side_out,
        "uf": unfold,
        "ux": side_unfold,
        "fn": from_near,
        "ff": from_far,
        "fold": fold_gain,
        "gu": gate_up,
        "dn": down,
        "rf": sum_far,
        "rn": sum_near,
        "fi": finish,
        "fs": finish_side,
        "l1": late_first,
        "l2": late_next,
        "co": combine,
    }
    for name, *at in ORDER:
        if name == "fold":
            weigh()
        steps[name](*at)

    out_ref[...] = total[...].astype(bf16)

    def blocks(chunk_list, count, ref, sem):
        for c in chunk_list:
            at = ref.at[c, 0 : count * block // (2 * mps), :]
            pltpu.make_async_copy(at, at, sem.at[c]).wait()

    whole = 2 * (segments * mps - 1)
    short = len(SIDES)
    blocks([c for c in range(chunks) if c not in EARLY], whole, rows, ag_send)
    blocks(EARLY, whole - short, rows, ag_send)
    blocks([c for c in range(chunks) if c not in LATE], whole, parts, rs_send)
    blocks(LATE, whole - short, parts, rs_send)
    for ref, sem, n in (
        (z_out, z_send, chunks),
        (b_out, b_send, chunks),
        (side, x_send, len(EARLY)),
        (late_out, y_send, len(LATE)),
    ):
        for c in range(n):
            at = ref.at[c, 0 : slots - per, :]
            pltpu.make_async_copy(at, at, sem.at[c]).wait()
    for ref, sem, n in ((side, side_send, len(EARLY)), (late_in, late_send, len(LATE))):
        for c in range(n):
            pltpu.make_async_copy(ref.at[c], ref.at[c], sem.at[c]).wait()


def body(tokens, routes, gate_weights, norm_gain, gate_proj, up_proj, down_proj):
    experts, segments, mps = (lax.axis_size(a) for a in ("expert", "segment", "mp"))
    tok, feat = tokens.shape[1:]
    capacity = min(tok, 20)
    chunks = -(-capacity // SLOTS)
    fold = feat // FOLDS
    slots = experts * FOLDS * SLOTS
    block = experts * SLOTS
    hid = down_proj.shape[1]
    width = feat * mps
    dims = (experts, segments, mps, tok, feat, chunks)
    bf16, f32 = jnp.bfloat16, jnp.float32
    early, late = max(len(EARLY), 1), max(len(LATE), 1)
    vmem, dma = pltpu.VMEM, pltpu.SemaphoreType.DMA
    out = pl.pallas_call(
        functools.partial(kernel, dims),
        out_shape=jax.ShapeDtypeStruct((tok, feat), bf16),
        in_specs=[pl.BlockSpec(memory_space=pltpu.VMEM)] * 4 + [pl.BlockSpec(memory_space=pl.ANY)] * 3,
        out_specs=pl.BlockSpec(memory_space=pltpu.VMEM),
        scratch_shapes=[
            vmem((hid, width), bf16),
            vmem((hid, width), bf16),
            vmem((hid, width), bf16),
            vmem((2, segments * block, hid), bf16),
            vmem((chunks, segments * block, width), bf16),
            vmem((chunks, segments * block, width), bf16),
            vmem((chunks, len(FAR), block, feat // 2), bf16),
            vmem((chunks, len(NEAR), block, feat), bf16),
            vmem((chunks, slots, fold), bf16),
            vmem((chunks, slots, fold), bf16),
            vmem((chunks, slots, fold), bf16),
            vmem((chunks, slots, fold), bf16),
            vmem((early, slots, len(SIDES) * fold // 2), bf16),
            vmem((early, slots, len(SIDES) * fold // 2), bf16),
            vmem((late, slots, len(SIDES) * fold // 2), bf16),
            vmem((late, slots, len(SIDES) * fold // 2), bf16),
            vmem((late, slots, len(SIDES) * fold // 2), bf16),
            vmem((slots, tok), f32),
            vmem((tok, slots), f32),
            vmem((tok, slots), f32),
            vmem((tok, feat), f32),
            dma((3,)),
            dma((chunks, IDS)),
            dma((chunks, IDS)),
            dma((chunks,)),
            dma((chunks,)),
            dma((chunks,)),
            dma((chunks,)),
            dma((chunks,)),
            dma((chunks,)),
            dma((early,)),
            dma((early, len(SIDES))),
            dma((early,)),
            dma((early,)),
            dma((late,)),
            dma((late,)),
            dma((late,)),
            dma((late, len(SIDES))),
        ],
        compiler_params=pltpu.CompilerParams(
            collective_id=0, has_side_effects=True, vmem_limit_bytes=60 * 1024 * 1024
        ),
        cost_estimate=pl.CostEstimate(
            flops=6 * chunks * segments * block * width * hid,
            bytes_accessed=6 * width * hid,
            transcendentals=chunks * segments * block * hid,
        ),
        name="expert_block",
    )(
        tokens[0],
        jnp.swapaxes(routes, 1, 2)[0],
        jnp.swapaxes(gate_weights, 1, 2)[0],
        norm_gain.reshape(-1, 128),
        jnp.swapaxes(gate_proj, 1, 2)[0],
        jnp.swapaxes(up_proj, 1, 2)[0],
        down_proj[0],
    )
    return out[None]


def solution(mesh):
    placed = (
        P("segment", "expert", "mp"),
        P("segment", "expert", None),
        P("segment", "expert", None),
        P(),
        P("expert", None, ("segment", "mp")),
        P("expert", None, ("segment", "mp")),
        P("expert", ("segment", "mp"), None),
    )
    return jax.shard_map(
        body, mesh=mesh, in_specs=placed, out_specs=P("segment", "expert", "mp"), check_vma=False
    )
```

```python
import functools
import jax
import jax.numpy as jnp
from jax import lax
from jax.experimental import pallas as pl
from jax.experimental.pallas import tpu as pltpu
from jax.sharding import PartitionSpec as P

EPSILON = 1e-06
SLOTS = 4
FOLDS = 4
MESH_IDS = pl.DeviceIdType.MESH

RING = (0, 1, -1, 2)
TURN = {0: -1, 1: 1, -1: -1, 2: 1}


def parent_a(dx, dy):
    if dy in (1, -1):
        return (dx, 0)
    if dy == 2:
        return (dx, TURN[dx])
    return (0, 0) if dx in (1, -1) else (1, 0)


def parent(half, node):
    dx, dy = node
    if half == 0:
        return parent_a(dx, dy)
    py, px = parent_a(dy, dx)
    return (px, py)


def level(node):
    return abs(node[0]) + abs(node[1])


NODES = [(dx, dy) for dx in RING for dy in RING if (dx, dy) != (0, 0)]
NEAR = [n for n in NODES if level(n) == 1]
FAR = [(half, n) for n in NODES if level(n) > 1 for half in (0, 1)]
NEAR_ID = {n: i for i, n in enumerate(NEAR)}
FAR_ID = {m: i for i, m in enumerate(FAR)}
IDS = len(NEAR) + len(FAR)


def children(half, node):
    return [n for h, n in FAR if h == half and parent(half, n) == node]


def depth_below(half, node):
    below = children(half, node)
    return 0 if not below else 1 + max(depth_below(half, n) for n in below)


def step_of(node, up):
    d = (up[0] - node[0], up[1] - node[1])
    return tuple({3: -1, -3: 1}.get(v, v) for v in d)


EARLY = (2, 3, 4)
LATE = (0, 1, 2)
SIDES = [(half, (0, d) if half else (d, 0)) for half in (0, 1) for d in (1, -1, 2)]
SIDE_ID = {m: i for i, m in enumerate(SIDES)}

ORDER = (
    ("mq", 2), ("z", 0), ("mq", 3), ("mq", 4), ("z", 1), ("z", 2), ("mf", 2), ("mf", 3), ("z", 3), ("mf", 4),
    ("uf", 0), ("zx", 2), ("uf", 1), ("zx", 3), ("z", 4), ("fn", 0, (1, 0)), ("fn", 0, (0, -1)),
    ("fn", 0, (0, 1)), ("uf", 2), ("fn", 0, (-1, 0)), ("uf", 3), ("ff", 0, 0, (2, 0)), ("fn", 1, (0, 1)),
    ("ff", 0, 0, (1, 1)), ("zx", 4), ("fn", 1, (1, 0)), ("ff", 0, 1, (0, 2)), ("fn", 1, (-1, 0)), ("fold",),
    ("ff", 0, 0, (-1, -1)), ("fn", 2, (0, 1)), ("ff", 0, 1, (1, 1)), ("fn", 3, (1, 0)), ("fn", 2, (0, -1)),
    ("ff", 0, 0, (2, 1)), ("fn", 3, (0, -1)), ("ff", 0, 1, (-1, -1)), ("ff", 0, 1, (1, 2)), ("fn", 2, (1, 0)),
    ("ff", 1, 1, (1, 1)), ("fn", 2, (-1, 0)), ("ff", 1, 1, (0, 2)), ("ff", 1, 0, (2, 0)), ("fn", 3, (0, 1)),
    ("fn", 3, (-1, 0)), ("ff", 1, 0, (1, 1)), ("fn", 1, (0, -1)), ("ux", 2), ("ff", 1, 0, (-1, -1)), ("gu", 0),
    ("ff", 1, 0, (2, 1)), ("ff", 1, 1, (1, 2)), ("ff", 1, 1, (-1, -1)), ("ux", 3), ("dn", 0, 2), ("dn", 0, 1),
    ("ff", 2, 1, (1, 1)), ("ff", 2, 0, (-1, -1)), ("ff", 2, 0, (1, 1)), ("ff", 2, 1, (1, 2)),
    ("ff", 2, 0, (2, 1)), ("ff", 2, 1, (-1, -1)), ("uf", 4), ("gu", 1), ("ff", 3, 1, (1, 1)),
    ("ff", 3, 0, (1, 1)), ("ff", 3, 0, (2, 1)), ("ff", 3, 0, (-1, -1)), ("ff", 3, 1, (1, 2)), ("ux", 4),
    ("dn", 0, -1), ("ff", 3, 1, (-1, -1)), ("rf", 0, 0, (-1, -1)), ("dn", 1, 2), ("dn", 1, 1), ("dn", 1, -1),
    ("dn", 0, 0), ("gu", 2), ("fn", 4, (0, -1)), ("ff", 4, 1, (-1, -1)), ("ff", 4, 0, (1, 1)),
    ("rf", 0, 1, (1, 1)), ("rf", 0, 0, (1, 1)), ("rf", 0, 1, (1, 2)), ("rn", 0, (0, -1)), ("fn", 4, (0, 1)),
    ("rf", 0, 0, (2, 1)), ("ff", 4, 0, (-1, -1)), ("dn", 1, 0), ("rf", 0, 1, (-1, -1)), ("ff", 4, 1, (1, 2)),
    ("ff", 4, 1, (1, 1)), ("ff", 4, 0, (2, 1)), ("fn", 4, (-1, 0)), ("dn", 2, 2), ("gu", 3),
    ("rf", 1, 0, (-1, -1)), ("rf", 1, 0, (1, 1)), ("rn", 1, (0, 1)), ("rf", 1, 1, (-1, -1)),
    ("rf", 1, 1, (1, 1)), ("dn", 2, 1), ("rf", 1, 1, (1, 2)), ("rf", 1, 0, (2, 1)), ("rn", 1, (1, 0)),
    ("dn", 2, -1), ("dn", 2, 0), ("rn", 2, (1, 0)), ("dn", 3, 2), ("dn", 3, 1), ("fs", 0), ("fn", 4, (1, 0)),
    ("gu", 4), ("rf", 2, 0, (1, 1)), ("rn", 1, (0, -1)), ("rf", 2, 0, (-1, -1)), ("dn", 4, 2),
    ("rf", 2, 1, (1, 2)), ("rn", 1, (-1, 0)), ("fs", 1), ("rf", 2, 1, (-1, -1)), ("rf", 2, 0, (2, 1)),
    ("rn", 2, (0, -1)), ("dn", 3, -1), ("rf", 2, 1, (1, 1)), ("rn", 0, (-1, 0)), ("rn", 2, (-1, 0)),
    ("dn", 4, 1), ("dn", 4, -1), ("rn", 2, (0, 1)), ("rf", 3, 0, (-1, -1)), ("rf", 3, 0, (2, 1)),
    ("rf", 4, 0, (2, 1)), ("rn", 0, (0, 1)), ("rf", 4, 1, (1, 2)), ("fi", 1), ("rf", 3, 1, (1, 2)),
    ("rf", 3, 1, (-1, -1)), ("dn", 4, 0), ("fs", 2), ("dn", 3, 0), ("rf", 4, 1, (1, 1)), ("rf", 4, 1, (0, 2)),
    ("rf", 4, 0, (1, 1)), ("rn", 0, (1, 0)), ("rf", 3, 0, (1, 1)), ("l1", 0), ("rf", 4, 0, (-1, -1)), ("fi", 2),
    ("rf", 4, 1, (-1, -1)), ("rf", 3, 0, (2, 0)), ("rn", 3, (0, -1)), ("rf", 4, 0, (2, 0)), ("rn", 4, (0, 1)),
    ("rf", 3, 1, (0, 2)), ("rf", 3, 1, (1, 1)), ("l1", 1), ("rn", 4, (0, -1)), ("rn", 4, (-1, 0)),
    ("rn", 4, (1, 0)), ("rn", 3, (1, 0)), ("rn", 3, (0, 1)), ("rn", 3, (-1, 0)), ("fi", 0), ("l1", 2),
    ("l2", 0), ("fi", 4), ("l2", 1), ("fi", 3), ("l2", 2), ("co", 0), ("co", 1), ("co", 4), ("co", 2),
    ("co", 3),
)


def kernel(
    dims,
    tokens_ref, routes_ref, gates_ref, gain_ref, gate_hbm, up_hbm, down_hbm,
    out_ref,
    gate_w, up_w, down_w, hidden, rows, parts, far_in, near_in,
    z_out, z_in, b_out, b_in, side, side_in, late_out, late_in, late_near, count, chosen_w, chosen_n, total,
    w_sem, ag_recv, rs_recv, ag_send, rs_send, z_send, z_recv, b_send, b_recv,
    side_send, side_recv, x_send, x_recv, y_send, y_recv, late_send, late_recv,
):
    experts, segments, mps, tok, feat, chunks = dims
    f32, bf16 = jnp.float32, jnp.bfloat16
    fold = feat // FOLDS
    half_w = feat // 2
    part = half_w // FOLDS
    per = FOLDS * SLOTS
    slots = experts * per
    block = experts * SLOTS
    seg, exp, mp = lax.axis_index("segment"), lax.axis_index("expert"), lax.axis_index("mp")

    def iota(shape, dim):
        return lax.broadcasted_iota(jnp.int32, shape, dim)

    barrier = pltpu.get_barrier_semaphore()

    @pl.loop(1, experts)
    def _(d):
        pl.semaphore_signal(
            barrier, inc=1, device_id={"expert": lax.rem(exp + d, experts)}, device_id_type=MESH_IDS
        )

    for d in (1, mps - 1):
        pl.semaphore_signal(
            barrier, inc=1, device_id={"mp": lax.rem(mp + d, mps)}, device_id_type=MESH_IDS
        )
    for d in (1, segments - 1):
        pl.semaphore_signal(
            barrier, inc=1, device_id={"segment": lax.rem(seg + d, segments)}, device_id_type=MESH_IDS
        )

    w_copies = [
        pltpu.make_async_copy(src, dst, w_sem.at[i])
        for i, (src, dst) in enumerate(((gate_hbm, gate_w), (up_hbm, up_w), (down_hbm, down_w)))
    ]
    for copy in w_copies:
        copy.start()

    row = iota((slots, tok), 0)
    first = routes_ref[0:1, :] == row // per
    second = routes_ref[1:2, :] == row // per
    named = jnp.logical_or(first, second)
    before = (iota((tok, tok), 0) < iota((tok, tok), 1)).astype(bf16)
    earlier = jnp.dot(named.astype(f32).astype(bf16), before, preferred_element_type=f32)
    count[...] = jnp.where(named, earlier, -1.0)
    row_fold = lax.rem(row, per) // SLOTS
    row_slot = lax.rem(row, SLOTS)

    @pl.loop(0, chunks)
    def _(c):
        fill = jnp.where(count[...] == (row_slot + SLOTS * c).astype(f32), 1.0, 0.0)
        picked = jnp.zeros((slots, fold), f32)
        for g in range(FOLDS):
            pick = jnp.where(row_fold == g, fill, 0.0).astype(bf16)
            picked = picked + jnp.dot(
                pick,
                jnp.concatenate(
                    [tokens_ref[:, h * half_w + g * part : h * half_w + (g + 1) * part] for h in (0, 1)],
                    axis=1,
                ),
                preferred_element_type=f32,
            )
        z_out[c] = picked.astype(bf16)

    pl.semaphore_wait(barrier, experts - 1 + 4)

    def z_go(out, got, send, recv, c, i=None):
        i = c if i is None else i
        base = pl.multiple_of(exp * per, per)
        pltpu.make_async_copy(
            out.at[i, pl.ds(base, per), :], got.at[i, pl.ds(base, per), :], recv.at[i]
        ).start()

        @pl.loop(1, experts)
        def _(d):
            other = lax.rem(exp + d, experts)
            pltpu.make_async_remote_copy(
                src_ref=out.at[i, pl.ds(pl.multiple_of(other * per, per), per), :],
                dst_ref=got.at[i, pl.ds(base, per), :],
                send_sem=send.at[i],
                recv_sem=recv.at[i],
                device_id={"expert": other},
                device_id_type=MESH_IDS,
            ).start()

    def sign(c):
        return 1 - 2 * (c % 2)

    def origin(c, node):
        s = sign(c)
        ox = lax.rem(seg + 2 * segments - s * node[0], segments)
        oy = lax.rem(mp + 2 * mps - s * node[1], mps)
        return ox, oy

    def spot(c, node, half=None):
        ox, oy = origin(c, node)
        r = pl.ds(pl.multiple_of(ox * block, block), block)
        if half is None:
            return r, pl.ds(pl.multiple_of(oy * feat, feat), feat)
        return r, pl.ds(pl.multiple_of(oy * feat + half * half_w, half_w), half_w)

    def hop(c, move):
        s = sign(c)
        if move[0] != 0:
            return {"segment": lax.rem(seg + segments + s * move[0], segments)}
        return {"mp": lax.rem(mp + mps + s * move[1], mps)}

    def near_half(c, node):
        if c in EARLY:
            return 1 if node[0] else 0
        return None

    def send_near(c):
        for node in NEAR:
            r, f = spot(c, (0, 0), near_half(c, node))
            pltpu.make_async_remote_copy(
                src_ref=rows.at[c, r, f],
                dst_ref=rows.at[c, r, f],
                send_sem=ag_send.at[c],
                recv_sem=ag_recv.at[c, NEAR_ID[node]],
                device_id=hop(c, node),
                device_id_type=MESH_IDS,
            ).start()

    def pass_on(c, half, node):
        for n in children(half, node):
            if c in EARLY and (half, n) in SIDE_ID:
                continue
            r, f = spot(c, node, half)
            pltpu.make_async_remote_copy(
                src_ref=rows.at[c, r, f],
                dst_ref=rows.at[c, r, f],
                send_sem=ag_send.at[c],
                recv_sem=ag_recv.at[c, len(NEAR) + FAR_ID[half, n]],
                device_id=hop(c, step_of(node, n)),
                device_id_type=MESH_IDS,
            ).start()

    def wait_far(c, half, node):
        r, f = spot(c, node, half)
        at = rows.at[c, r, f]
        pltpu.make_async_copy(at, at, ag_recv.at[c, len(NEAR) + FAR_ID[half, node]]).wait()

    def from_near(c, node):
        only = near_half(c, node)
        r, f = spot(c, node, only)
        at = rows.at[c, r, f]
        pltpu.make_async_copy(at, at, ag_recv.at[c, NEAR_ID[node]]).wait()
        for half in (0, 1) if only is None else (only,):
            pass_on(c, half, node)

    def from_far(c, half, node):
        wait_far(c, half, node)
        pass_on(c, half, node)

    def unfold(c):
        pltpu.make_async_copy(z_in.at[c], z_in.at[c], z_recv.at[c]).wait()
        spread(c, z_in[c], [(0, (0, 0)), (1, (0, 0))])
        send_near(c)

    def spread(c, got, places):
        r_, q_ = iota((block, slots), 0), iota((block, slots), 1)
        place = (r_ // SLOTS) * per + lax.rem(r_, SLOTS)
        for g in range(FOLDS):
            pick = jnp.where(q_ == place + g * SLOTS, 1.0, 0.0).astype(bf16)
            whole = jnp.dot(pick, got, preferred_element_type=f32).astype(bf16)
            for i, (half, node) in enumerate(places):
                ox, oy = origin(c, node)
                rows[
                    c,
                    pl.ds(pl.multiple_of(ox * block, block), block),
                    pl.ds(pl.multiple_of(oy * feat + half * half_w + g * part, part), part),
                ] = whole[:, i * part : (i + 1) * part]

    def side_copy(c, half, node, own):
        e, i = EARLY.index(c), SIDE_ID[half, node]
        up = (0, 0) if own else parent(half, node)
        lane = lambda k: pl.ds(k * part, part)
        src = z_out.at[c, :, lane(half)] if own else side.at[e, :, lane(SIDE_ID[half, up])]
        return pltpu.make_async_remote_copy(
            src_ref=src,
            dst_ref=side.at[e, :, lane(i)],
            send_sem=side_send.at[e],
            recv_sem=side_recv.at[e, i],
            device_id=hop(c, step_of(up, node)),
            device_id_type=MESH_IDS,
        )

    def side_wait(c, half, node):
        e, i = EARLY.index(c), SIDE_ID[half, node]
        at = side.at[e, :, pl.ds(i * part, part)]
        pltpu.make_async_copy(at, at, side_recv.at[e, i]).wait()

    def side_first(c):
        for half, node in SIDES:
            if level(node) == 1:
                side_copy(c, half, node, True).start()

    def side_next(c):
        for half, node in SIDES:
            if level(node) == 2:
                side_wait(c, half, parent(half, node))
                side_copy(c, half, node, False).start()

    def side_out(c):
        for half, node in SIDES:
            if level(node) == 2 or node not in [parent(h, n) for h, n in SIDES if h == half]:
                side_wait(c, half, node)
        z_go(side, side_in, x_send, x_recv, c, EARLY.index(c))

    def side_unfold(c):
        e = EARLY.index(c)
        pltpu.make_async_copy(side_in.at[e], side_in.at[e], x_recv.at[e]).wait()
        spread(c, side_in[e], SIDES)
        for half, node in SIDES:
            pass_on(c, half, node)

    nt = (((1,), (1,)), ((), ()))

    def fold_gain():
        for copy in w_copies:
            copy.wait()

        @pl.loop(0, feat * mps // 128)
        def _(i):
            cols = pl.ds(pl.multiple_of(i * 128, 128), 128)
            gain = gain_ref[pl.ds(i, 1), :]
            for w in (gate_w, up_w):
                w[:, cols] = (w[:, cols].astype(f32) * gain).astype(bf16)

    def gate_up(c):
        for half, node in FAR:
            if not children(half, node):
                wait_far(c, half, node)
        x = rows[c]
        gate = lax.dot_general(x, gate_w[...], nt, preferred_element_type=f32)
        up = lax.dot_general(x, up_w[...], nt, preferred_element_type=f32)
        squares = jnp.zeros((segments * block, 128), f32)
        for i in range(feat * mps // 128):
            v = rows[c, :, i * 128 : (i + 1) * 128].astype(f32)
            squares = squares + v * v
        mean = jnp.sum(squares, axis=1, keepdims=True) / (feat * mps)
        scale = lax.rsqrt(mean + EPSILON)
        gate = gate * scale
        hidden[c % 2] = (gate / (1.0 + jnp.exp(-gate)) * (up * scale)).astype(bf16)

    def down(c, dy):
        oy = lax.rem(mp + 2 * mps - sign(c) * dy, mps)

        @pl.loop(0, 2)
        def _(i):
            cols = pl.ds(pl.multiple_of(oy * feat + i * half_w, half_w), half_w)
            parts[c, :, cols] = jnp.dot(
                hidden[c % 2], down_w[:, cols], preferred_element_type=f32
            ).astype(bf16)

        for half, node in FAR:
            if node[1] == dy and not children(half, node):
                send_far(c, half, node)

    def add_up(c, half, node):
        below = [FAR_ID[half, n] for n in children(half, node) if not (c in LATE and (half, n) in SIDE_ID)]
        for i in below:
            at = far_in.at[c, i]
            pltpu.make_async_copy(at, at, rs_recv.at[c, len(NEAR) + i]).wait()
        ox, oy = origin(c, node)
        f = pl.ds(pl.multiple_of(oy * feat + half * half_w, half_w), half_w)

        @pl.loop(0, block // 16)
        def _(k):
            r = pl.ds(pl.multiple_of(ox * block + k * 16, 16), 16)
            acc = parts[c, r, f].astype(f32)
            for i in below:
                acc = acc + far_in[c, i, pl.ds(pl.multiple_of(k * 16, 16), 16), :].astype(f32)
            parts[c, r, f] = acc.astype(bf16)

    def send_far(c, half, node):
        r, f = spot(c, node, half)
        i = FAR_ID[half, node]
        pltpu.make_async_remote_copy(
            src_ref=parts.at[c, r, f],
            dst_ref=far_in.at[c, i],
            send_sem=rs_send.at[c],
            recv_sem=rs_recv.at[c, len(NEAR) + i],
            device_id=hop(c, step_of(node, parent(half, node))),
            device_id_type=MESH_IDS,
        ).start()

    def sum_far(c, half, node):
        add_up(c, half, node)
        send_far(c, half, node)

    def sum_near(c, node):
        only = (1 if node[0] else 0) if c in LATE else None
        for half in (0, 1) if only is None else (only,):
            if children(half, node):
                add_up(c, half, node)
        r, f = spot(c, node, only)
        at = near_in.at[c, NEAR_ID[node]]
        if only is not None:
            at = near_in.at[c, NEAR_ID[node], :, pl.ds(only * half_w, half_w)]
        pltpu.make_async_remote_copy(
            src_ref=parts.at[c, r, f],
            dst_ref=at,
            send_sem=rs_send.at[c],
            recv_sem=rs_recv.at[c, NEAR_ID[node]],
            device_id=hop(c, (-node[0], -node[1])),
            device_id_type=MESH_IDS,
        ).start()

    def gather_up(pieces):
        q_, r_ = iota((slots, block), 0), iota((slots, block), 1)
        place = (r_ // SLOTS) * per + lax.rem(r_, SLOTS)
        back = None
        for g in range(FOLDS):
            pick = jnp.where(q_ == place + g * SLOTS, 1.0, 0.0).astype(bf16)
            add = jnp.dot(pick, pieces(g), preferred_element_type=f32)
            back = add if back is None else back + add
        return back.astype(bf16)

    def finish(c):
        late = c in LATE
        for node in NEAR:
            i = NEAR_ID[node]
            at = near_in.at[c, i]
            if late:
                at = near_in.at[c, i, :, pl.ds((1 if node[0] else 0) * half_w, half_w)]
            pltpu.make_async_copy(at, at, rs_recv.at[c, i]).wait()
        ox = pl.ds(pl.multiple_of(seg * block, block), block)

        def pieces(g):
            both = []
            for half in (0, 1):
                at = half * half_w + g * part
                acc = parts[c, ox, pl.ds(pl.multiple_of(mp * feat + at, part), part)].astype(f32)
                for node in NEAR:
                    if not late or half == (1 if node[0] else 0):
                        acc = acc + near_in[c, NEAR_ID[node], :, at : at + part].astype(f32)
                both.append(acc.astype(bf16))
            return jnp.concatenate(both, axis=1)

        b_out[c] = gather_up(pieces)
        z_go(b_out, b_in, b_send, b_recv, c)

    def finish_side(c):
        e = LATE.index(c)
        for half, node in SIDES:
            add_up(c, half, node)

        def pieces(g):
            whole = []
            for half, node in SIDES:
                ox, oy = origin(c, node)
                whole.append(
                    parts[
                        c,
                        pl.ds(pl.multiple_of(ox * block, block), block),
                        pl.ds(pl.multiple_of(oy * feat + half * half_w + g * part, part), part),
                    ]
                )
            return jnp.concatenate(whole, axis=1)

        late_out[e] = gather_up(pieces)
        z_go(late_out, late_in, y_send, y_recv, c, e)

    def late_copy(c, half, node):
        e, i = LATE.index(c), SIDE_ID[half, node]
        up = parent(half, node)
        return pltpu.make_async_remote_copy(
            src_ref=late_in.at[e, :, pl.ds(i * part, part)],
            dst_ref=late_near.at[e, :, pl.ds(i * part, part)],
            send_sem=late_send.at[e],
            recv_sem=late_recv.at[e, i],
            device_id=hop(c, step_of(node, up)),
            device_id_type=MESH_IDS,
        )

    def late_wait(c, half, node):
        e, i = LATE.index(c), SIDE_ID[half, node]
        at = late_near.at[e, :, pl.ds(i * part, part)]
        pltpu.make_async_copy(at, at, late_recv.at[e, i]).wait()

    def late_first(c):
        e = LATE.index(c)
        pltpu.make_async_copy(late_in.at[e], late_in.at[e], y_recv.at[e]).wait()
        inner = [(h, parent(h, n)) for h, n in SIDES if level(n) == 2]
        for half, node in SIDES:
            if (half, node) not in inner:
                late_copy(c, half, node).start()

    def late_next(c):
        e = LATE.index(c)
        for half, node in SIDES:
            if level(node) == 2:
                late_wait(c, half, node)
                up = parent(half, node)
                f, n = (slice(SIDE_ID[half, v] * part, (SIDE_ID[half, v] + 1) * part) for v in (node, up))
                late_in[e, :, n] = (
                    late_in[e, :, n].astype(f32) + late_near[e, :, f].astype(f32)
                ).astype(bf16)
                late_copy(c, half, up).start()

    lane_fold = lax.rem(iota((tok, slots), 1), per) // SLOTS
    lane_slot = lax.rem(iota((tok, slots), 1), SLOTS)

    def combine(c):
        pltpu.make_async_copy(b_in.at[c], b_in.at[c], b_recv.at[c]).wait()
        got = b_in[c]
        if c in LATE:
            e = LATE.index(c)
            lanes = []
            for half in (0, 1):
                acc = got[:, half * part : (half + 1) * part].astype(f32)
                for h, node in SIDES:
                    if h == half and level(node) == 1:
                        late_wait(c, half, node)
                        i = SIDE_ID[half, node]
                        acc = acc + late_near[e, :, i * part : (i + 1) * part].astype(f32)
                lanes.append(acc.astype(bf16))
            got = jnp.concatenate(lanes, axis=1)
        share = jnp.where(chosen_n[...] == (lane_slot + SLOTS * c).astype(f32), chosen_w[...], 0.0)
        for g in range(FOLDS):
            mine = jnp.where(lane_fold == g, share, 0.0)
            high = mine.astype(bf16)
            low = (mine - high.astype(f32)).astype(bf16)
            add = jnp.dot(high, got, preferred_element_type=f32) + jnp.dot(
                low, got, preferred_element_type=f32
            )
            for half in (0, 1):
                at = half * half_w + g * part
                total[:, at : at + part] += add[:, half * part : (half + 1) * part]

    def weigh():
        total[...] = tokens_ref[...].astype(f32)
        weight = jnp.where(first, gates_ref[0:1, :], 0.0) + jnp.where(second, gates_ref[1:2, :], 0.0)
        chosen_w[...] = jnp.transpose(weight)
        chosen_n[...] = jnp.transpose(count[...])

    steps = {
        "z": lambda c: z_go(z_out, z_in, z_send, z_recv, c),
        "mq": side_first,
        "mf": side_next,
        "zx": side_out,
        "uf": unfold,
        "ux": side_unfold,
        "fn": from_near,
        "ff": from_far,
        "fold": fold_gain,
        "gu": gate_up,
        "dn": down,
        "rf": sum_far,
        "rn": sum_near,
        "fi": finish,
        "fs": finish_side,
        "l1": late_first,
        "l2": late_next,
        "co": combine,
    }
    for name, *at in ORDER:
        if name == "fold":
            weigh()
        steps[name](*at)

    out_ref[...] = total[...].astype(bf16)

    def blocks(chunk_list, count, ref, sem):
        for c in chunk_list:
            at = ref.at[c, 0 : count * block // (2 * mps), :]
            pltpu.make_async_copy(at, at, sem.at[c]).wait()

    whole = 2 * (segments * mps - 1)
    short = len(SIDES)
    blocks([c for c in range(chunks) if c not in EARLY], whole, rows, ag_send)
    blocks(EARLY, whole - short, rows, ag_send)
    blocks([c for c in range(chunks) if c not in LATE], whole, parts, rs_send)
    blocks(LATE, whole - short, parts, rs_send)
    for ref, sem, n in (
        (z_out, z_send, chunks),
        (b_out, b_send, chunks),
        (side, x_send, len(EARLY)),
        (late_out, y_send, len(LATE)),
    ):
        for c in range(n):
            at = ref.at[c, 0 : slots - per, :]
            pltpu.make_async_copy(at, at, sem.at[c]).wait()
    for ref, sem, n in ((side, side_send, len(EARLY)), (late_in, late_send, len(LATE))):
        for c in range(n):
            pltpu.make_async_copy(ref.at[c], ref.at[c], sem.at[c]).wait()


def body(tokens, routes, gate_weights, norm_gain, gate_proj, up_proj, down_proj):
    experts, segments, mps = (lax.axis_size(a) for a in ("expert", "segment", "mp"))
    tok, feat = tokens.shape[1:]
    capacity = min(tok, 20)
    chunks = -(-capacity // SLOTS)
    fold = feat // FOLDS
    slots = experts * FOLDS * SLOTS
    block = experts * SLOTS
    hid = down_proj.shape[1]
    width = feat * mps
    dims = (experts, segments, mps, tok, feat, chunks)
    bf16, f32 = jnp.bfloat16, jnp.float32
    early, late = max(len(EARLY), 1), max(len(LATE), 1)
    vmem, dma = pltpu.VMEM, pltpu.SemaphoreType.DMA
    out = pl.pallas_call(
        functools.partial(kernel, dims),
        out_shape=jax.ShapeDtypeStruct((tok, feat), bf16),
        in_specs=[pl.BlockSpec(memory_space=pltpu.VMEM)] * 4 + [pl.BlockSpec(memory_space=pl.ANY)] * 3,
        out_specs=pl.BlockSpec(memory_space=pltpu.VMEM),
        scratch_shapes=[
            vmem((hid, width), bf16),
            vmem((hid, width), bf16),
            vmem((hid, width), bf16),
            vmem((2, segments * block, hid), bf16),
            vmem((chunks, segments * block, width), bf16),
            vmem((chunks, segments * block, width), bf16),
            vmem((chunks, len(FAR), block, feat // 2), bf16),
            vmem((chunks, len(NEAR), block, feat), bf16),
            vmem((chunks, slots, fold), bf16),
            vmem((chunks, slots, fold), bf16),
            vmem((chunks, slots, fold), bf16),
            vmem((chunks, slots, fold), bf16),
            vmem((early, slots, len(SIDES) * fold // 2), bf16),
            vmem((early, slots, len(SIDES) * fold // 2), bf16),
            vmem((late, slots, len(SIDES) * fold // 2), bf16),
            vmem((late, slots, len(SIDES) * fold // 2), bf16),
            vmem((late, slots, len(SIDES) * fold // 2), bf16),
            vmem((slots, tok), f32),
            vmem((tok, slots), f32),
            vmem((tok, slots), f32),
            vmem((tok, feat), f32),
            dma((3,)),
            dma((chunks, IDS)),
            dma((chunks, IDS)),
            dma((chunks,)),
            dma((chunks,)),
            dma((chunks,)),
            dma((chunks,)),
            dma((chunks,)),
            dma((chunks,)),
            dma((early,)),
            dma((early, len(SIDES))),
            dma((early,)),
            dma((early,)),
            dma((late,)),
            dma((late,)),
            dma((late,)),
            dma((late, len(SIDES))),
        ],
        compiler_params=pltpu.CompilerParams(
            collective_id=0, has_side_effects=True, vmem_limit_bytes=60 * 1024 * 1024
        ),
        cost_estimate=pl.CostEstimate(
            flops=6 * chunks * segments * block * width * hid,
            bytes_accessed=6 * width * hid,
            transcendentals=chunks * segments * block * hid,
        ),
        name="expert_block",
    )(
        tokens[0],
        jnp.swapaxes(routes, 1, 2)[0],
        jnp.swapaxes(gate_weights, 1, 2)[0],
        norm_gain.reshape(-1, 128),
        jnp.swapaxes(gate_proj, 1, 2)[0],
        jnp.swapaxes(up_proj, 1, 2)[0],
        down_proj[0],
    )
    return out[None]


def solution(mesh):
    placed = (
        P("segment", "expert", "mp"),
        P("segment", "expert", None),
        P("segment", "expert", None),
        P(),
        P("expert", None, ("segment", "mp")),
        P("expert", None, ("segment", "mp")),
        P("expert", ("segment", "mp"), None),
    )
    return jax.shard_map(
        body, mesh=mesh, in_specs=placed, out_specs=P("segment", "expert", "mp"), check_vma=False
    )
```
